512 devices in a mesh: grp: 16 (over x, y), gx: 16 (over z_lo, core), gy: 2 (over z_hi).
Axes of the slice: x: 4, y: 4, z: 16 (z_hi: 2, z_lo: 8; z = z_hi * 8 + z_lo), core: 2. Of those that a mesh axis runs over, the one named last changes fastest.
Arguments:
- air: float32 [2, 32, 512, 1536], P(None, None, ('grp', 'gx'), 'gy'), may hold values from -6 to 6
- kdiff: float32 [512, 1536], P(('grp', 'gx'), 'gy'), may hold values from 0.02 to 0.2
- u_wind: float32 [32], replicated, may hold values from -0.15 to 0.15
- v_wind: float32 [32], replicated, may hold values from -0.15 to 0.15
- elev: float32 [2048, 6144], P(('grp', 'gx'), 'gy'), may hold values from 0 to 1
- cond: float32 [2048, 6144], P(('grp', 'gx'), 'gy'), may hold values from 0.01 to 0.1
- rain_factor: float32 [2048, 6144], P(('grp', 'gx'), 'gy'), may hold values from 0.5 to 2
- land_mask: int32 [2048, 6144], P(('grp', 'gx'), 'gy'), may hold values 0 or 1
- flow_code: int32 [2048, 6144], P(('grp', 'gx'), 'gy'), may hold values from 0 to 3
- depth_init: float32 [2048, 6144], P(('grp', 'gx'), 'gy'), may hold values from 0 to 0.5
- soil_init: float32 [2048, 6144], P(('grp', 'gx'), 'gy'), may hold values from 0 to 1
- link_cell: int32 [131072], P(('grp', 'gx', 'gy')), may hold values from 0 to 24575
- link_down: int32 [131072], P(('grp', 'gx', 'gy')), may hold values from 0 to 512, as said below
- link_flow: float32 [131072], P(('grp', 'gx', 'gy')), may hold values from 0 to 1
Outputs:
- air_out: float32 [2, 32, 512, 1536], P(None, None, ('grp', 'gx'), 'gy')
- depth_out: float32 [2048, 6144], P(('grp', 'gx'), 'gy')
- soil_coarse: float32 [512, 1536], P(('grp', 'gx'), 'gy')
- channel_flow: float32 [131072], P(('grp', 'gx', 'gy'))
The draws below stay inside these ranges and needn't reach their ends.
Inputs may be any that keep to these rules, and one draw needn't show every extreme that they name: `link_down`: for a link of device d with value v: v < 256 names link v of the same device, 256 <= v < 512 names link v - 256 of the device with the next grp+gx index and the same gy, 512 is an outlet; devices of the last grp+gx index hold no values in the middle range. `link_cell`: A cell of the link's own device's block of the terrain grid, as row * 3072 + column.
All inputs are finite; a program needn't handle non-finite values. No bound on the sum of `land_mask` on one device may be relied on, other than what follows from the above.
Results may differ from the reference program's by a relative error of at most 0.00025.
Values sent between devices are 32-bit elements; how exact they have to be, the bound alone decides.
No kernel may reach another device: no remote copies, remote signals or barrier semaphores. Data moves between devices by JAX's collectives and lax.ppermute only.
A program may use at most 64 MiB of HBM per device.

```python
import math
import jax
import jax.numpy as jnp

LEV = 32
ASTEPS = 2
HSTEPS = 4
COUPLE = 2
LINKS_DEV = 256
AX = 512
AY = 1536
HROW = 8
HCOL = 3072
HX = 2048
HY = 6144
LINKS = 131072
N_GRP = 16
N_GX = 16
N_GY = 2


def draw_link_down(key, part):
    key = jax.random.fold_in(key, 7)
    index = jnp.arange(LINKS, dtype=jnp.int32)
    row = index // LINKS_DEV // N_GY
    value = jax.random.randint(key, (LINKS,), 0, 2 * LINKS_DEV + 1, dtype=jnp.int32)
    last = row == N_GRP * N_GX - 1
    middle = (value >= LINKS_DEV) & (value < 2 * LINKS_DEV)
    value = jnp.where(last & middle, value - LINKS_DEV, value)
    value = value.at[0].set(2 * LINKS_DEV)
    return value.astype(jnp.int32)


def set_ends(entries, rng, smallest, high):
    shape = entries.shape
    place = [jax.random.randint(jax.random.fold_in(rng, axis), (), 0, shape[axis]) for axis in range(len(shape))]
    entries = entries.at[tuple(place)].set(smallest)
    longest = shape.index(max(shape))
    place[longest] = (place[longest] + 1) % shape[longest]
    return entries.at[tuple(place)].set(high)


def block_scale(key, shape, shards, least, top_value):
    def one(dim, parts):
        heights = jax.random.uniform(jax.random.fold_in(jax.random.fold_in(key, 6), dim), (parts,), jnp.float32, least / len(shards), top_value / len(shards))
        return jnp.repeat(jnp.exp(heights), shape[dim] // parts).reshape((-1,) + (1,) * (len(shape) - dim - 1))

    loudness = one(*shards[0])
    for cut in shards[1:]:
        loudness = loudness * one(*cut)
    return loudness


def noise(key, extent, width, limit, split=(), kind=jnp.bfloat16):
    factor_of = block_scale(key, extent, split, -0.22, 0.18) if split else 1.0
    entries = jax.random.normal(key, extent, jnp.float32) * width * factor_of
    return jnp.minimum(jnp.maximum(entries, -limit), limit).astype(kind)


def setup_inputs(seed: int = 0) -> dict:
    splits = jax.random.split(jax.random.key(seed), 15)
    air = noise(splits[0], (2, LEV, AX, AY), 1.0, 6.0, ((2, 256), (3, 2)), jnp.float32)
    kdiff = jnp.clip(jnp.exp(math.log(0.2) - 2.3025851 * jax.random.uniform(splits[1], (AX, AY), jnp.float32) ** block_scale(splits[1], (AX, AY), ((0, 256), (1, 2)), -0.2, 0.2)), 0.02, 0.2)
    u_wind = jnp.clip(jax.random.uniform(splits[2], (LEV,), jnp.float32, -0.15, 0.15), -0.15, 0.15)
    v_wind = jnp.clip(jax.random.uniform(splits[3], (LEV,), jnp.float32, -0.15, 0.15), -0.15, 0.15)
    elev = jnp.clip(1.0 * jax.random.uniform(splits[4], (HX, HY), jnp.float32) ** block_scale(splits[4], (HX, HY), ((0, 256), (1, 2)), -0.2, 0.2), 0.0, 1.0)
    cond = jnp.clip(jnp.exp(math.log(0.1) - 2.3025851 * jax.random.uniform(splits[5], (HX, HY), jnp.float32) ** block_scale(splits[5], (HX, HY), ((0, 256), (1, 2)), -0.2, 0.2)), 0.01, 0.1)
    rain_factor = jnp.clip(jnp.exp(math.log(2.0) - 1.3862944 * jax.random.uniform(splits[6], (HX, HY), jnp.float32) ** block_scale(splits[6], (HX, HY), ((0, 256), (1, 2)), -0.2, 0.2)), 0.5, 2.0)
    land_mask = set_ends((jax.random.randint(splits[7], (HX, HY), 0, 10) < 9).astype(jnp.int32), jax.random.fold_in(splits[7], 1), 0, 1)
    flow_code = set_ends(jax.random.randint(splits[8], (HX, HY), 0, 4), jax.random.fold_in(splits[8], 1), 0, 3).astype(jnp.int32)
    depth_init = jnp.clip(0.5 * jax.random.uniform(splits[9], (HX, HY), jnp.float32) ** block_scale(splits[9], (HX, HY), ((0, 256), (1, 2)), -0.2, 0.2), 0.0, 0.5)
    soil_init = jnp.clip(1.0 * jax.random.uniform(splits[10], (HX, HY), jnp.float32) ** block_scale(splits[10], (HX, HY), ((0, 256), (1, 2)), -0.2, 0.2), 0.0, 1.0)
    link_cell = set_ends(jax.random.randint(splits[11], (LINKS,), 0, HROW * HCOL), jax.random.fold_in(splits[11], 1), 0, (HROW * HCOL) - 1).astype(jnp.int32)
    link_down = draw_link_down(jax.random.fold_in(splits[14], 71), 0)
    link_flow = jnp.clip(1.0 * jax.random.uniform(splits[13], (LINKS,), jnp.float32) ** block_scale(splits[13], (LINKS,), ((0, 512),), -0.2, 0.2), 0.0, 1.0)
    return dict(air=air, kdiff=kdiff, u_wind=u_wind, v_wind=v_wind, elev=elev, cond=cond, rain_factor=rain_factor, land_mask=land_mask, flow_code=flow_code, depth_init=depth_init, soil_init=soil_init, link_cell=link_cell, link_down=link_down, link_flow=link_flow)


def atmos_update(air, kdiff, u_wind, v_wind):
    padded = jnp.pad(air, ((0, 0), (0, 0), (1, 1), (1, 1)))
    centre = padded[:, :, 1:-1, 1:-1]
    north = padded[:, :, :-2, 1:-1]
    south = padded[:, :, 2:, 1:-1]
    west = padded[:, :, 1:-1, :-2]
    east = padded[:, :, 1:-1, 2:]
    lap = north + south + west + east - 4.0 * centre
    return centre + kdiff * lap - 0.5 * u_wind[:, None, None] * (east - west) - 0.5 * v_wind[:, None, None] * (south - north)


def reference(air, kdiff, u_wind, v_wind, elev, cond, rain_factor, land_mask, flow_code, depth_init, soil_init, link_cell, link_down, link_flow):
    depth = depth_init
    soil = soil_init
    flow = link_flow
    mask = land_mask.astype(jnp.float32)
    index = jnp.arange(LINKS, dtype=jnp.int32)
    device = index // LINKS_DEV
    target = jnp.where(link_down < LINKS_DEV, device * LINKS_DEV + link_down,
                       jnp.where(link_down < 2 * LINKS_DEV, (device + N_GY) * LINKS_DEV + link_down - LINKS_DEV, LINKS))
    target = target.astype(jnp.int32)
    cell_row = (device // N_GY) * HROW + link_cell // HCOL
    cell_col = (device % N_GY) * HCOL + link_cell % HCOL
    codes = jnp.pad(flow_code, 1)
    soil_coarse = jnp.zeros((AX, AY), jnp.float32)
    for cycle in range(COUPLE):
        for step in range(ASTEPS):
            air = atmos_update(air, kdiff, u_wind, v_wind)
        ground = air[1, 0]
        rain = 0.05 * ground * ground
        air = air.at[1, 0].add(-rain)
        rain_fine = jnp.repeat(jnp.repeat(rain, 4, axis=0), 4, axis=1) * rain_factor
        for step in range(HSTEPS):
            eta = elev + depth
            out = 0.2 * depth
            pe = jnp.pad(eta, 1)
            po = jnp.pad(out, 1)
            inflow = (po[1:-1, :-2] * (codes[1:-1, :-2] == 0) + po[1:-1, 2:] * (codes[1:-1, 2:] == 2)
                      + po[2:, 1:-1] * (codes[2:, 1:-1] == 1) + po[:-2, 1:-1] * (codes[:-2, 1:-1] == 3))
            lap = pe[:-2, 1:-1] + pe[2:, 1:-1] + pe[1:-1, :-2] + pe[1:-1, 2:] - 4.0 * eta
            lateral = 0.1 * depth[cell_row, cell_col]
            routed = jax.ops.segment_sum(flow, target, num_segments=LINKS + 1)[:LINKS]
            flow = flow + 0.5 * (routed - flow) + lateral
            soil = soil + 0.05 * mask * depth - 0.02 * soil
            depth = mask * (depth + rain_fine - out + inflow - 0.05 * depth + cond * lap)
        soil_coarse = soil.reshape(AX, 4, AY, 4).mean(axis=(1, 3))
        air = air.at[1, 0].add(0.1 * soil_coarse * jax.nn.sigmoid(air[0, 0]))
    return air, depth, soil_coarse, flow
```

```python
import jax
import jax.numpy as jnp
from jax import lax
from jax.experimental import pallas as pl
from jax.experimental.pallas import tpu as pltpu
from jax.sharding import PartitionSpec as P

ASTEPS = 2
HSTEPS = 4
COUPLE = 2
STEPS = HSTEPS * COUPLE

F32 = jnp.float32
BF16 = jnp.bfloat16
AXES = ("grp", "gx", "gy")
PARAMS = pltpu.CompilerParams(vmem_limit_bytes=48 * 1024 * 1024)

LINKS = 256
TR = 8
TC = 3072
TW = TC + 128
AC = 768
AW = AC + 128
FL = 64
Q0 = 32


def exchange(value, partner):
    pairs = []
    for r in range(256):
        for g in range(2):
            t, h = partner(r, g)
            if 0 <= t < 256:
                pairs.append((r * 2 + g, t * 2 + h))
    return lax.ppermute(value, AXES, pairs)


def outer(r):
    return r + 1 if r % 2 else r - 1


def pair_swap(value):
    return exchange(value, lambda r, g: (r ^ 1, g))


def chip_swap(value):
    return exchange(value, lambda r, g: (outer(r), g))


def near_swap(value):
    return exchange(
        value, lambda r, g: (outer(r), g if outer(r) // 16 == r // 16 else 1 - g)
    )


def gy_swap(value):
    return exchange(value, lambda r, g: (r, 1 - g))


def grp_shift(value):
    return exchange(value, lambda r, g: (r + 16, g))


def vmem():
    return pl.BlockSpec(memory_space=pltpu.VMEM)


def smem():
    return pl.BlockSpec(memory_space=pltpu.SMEM)


def call(body, out_shapes, scalars, arrays, scratch=()):
    return pl.pallas_call(
        body,
        out_shape=[jax.ShapeDtypeStruct(s, F32) for s in out_shapes],
        in_specs=[smem()] * len(scalars) + [vmem()] * len(arrays),
        out_specs=[vmem() for _ in out_shapes],
        scratch_shapes=[pltpu.VMEM(s, F32) for s in scratch],
        compiler_params=PARAMS,
    )(*scalars, *arrays)


def pack_body(info, air, kd, elev, cond, rf, mask, code, depth, soil, airc, msg_in, msg_out, strip):
    odd = info[0] == 1
    right = info[1] == 1
    for r in range(2):
        airc[r] = air[:, r, :]
    msg_in[...] = jnp.zeros((32, TC), F32)
    msg_out[...] = jnp.zeros((24, TC), F32)
    for ref, off, n in (
        (elev, 0, 4),
        (code, 4, 4),
        (depth, 8, 4),
        (cond, 12, 3),
        (rf, 15, 3),
        (mask, 18, 3),
    ):
        top = ref[0:n, :].astype(F32)
        low = ref[TR - n : TR, :].astype(F32)
        msg_in[off : off + n, :] = jnp.where(odd, top, low)
        msg_out[off : off + n, :] = jnp.where(odd, low, top)
    for msg in (msg_in, msg_out):
        for r in range(2):
            msg[21:22, r * AC : (r + 1) * AC] = airc[r, Q0 : Q0 + 1, :]
            msg[21:22, (2 + r) * AC : (3 + r) * AC] = airc[r, 0:1, :]
            msg[22:23, r * AC : (r + 1) * AC] = kd[r : r + 1, :]
    blocks = []
    for ref in (elev, cond, rf, mask, code, depth, soil):
        blocks.append(jnp.where(right, ref[:, 0:128], ref[:, TC - 128 : TC]).astype(F32))
    kblock = jnp.where(right, kd[:, 0:128], kd[:, AC - 128 : AC])
    square = jnp.concatenate(blocks + [kblock, jnp.zeros((70, 128), F32)], axis=0).T
    strip[0:16, :] = jnp.where(right, square[0:16], square[112:128])
    ablock = jnp.concatenate(
        [jnp.where(right, airc[r, :, 0:128], airc[r, :, AC - 128 : AC]) for r in range(2)], axis=0
    ).T
    strip[16:24, :] = jnp.where(right, ablock[0:8], ablock[120:128])
    for b in range(3):
        msg_in[24:32, b * 128 : (b + 1) * 128] = strip[8 * b : 8 * b + 8, :]


def land_strip(strip, right):
    zero = jnp.zeros((112, 128), F32)
    s = strip[0:16, :]
    return jnp.where(
        right, jnp.concatenate([zero, s], axis=0), jnp.concatenate([s, zero], axis=0)
    ).T


def air_strip(strip, right):
    zero = jnp.zeros((120, 128), F32)
    s = strip[16:24, :]
    return jnp.where(
        right, jnp.concatenate([zero, s], axis=0), jnp.concatenate([s, zero], axis=0)
    ).T


def lanes_inside(right, rows):
    lane = lax.broadcasted_iota(jnp.int32, (rows, AW), 1)
    edge = jnp.where(right, AW - 8, AC)
    halo = (lane >= edge) & (lane < edge + 8)
    return jnp.where((lane < AC) | halo, 1.0, 0.0).astype(F32)


def ring_mask(r, right):
    row = lax.broadcasted_iota(jnp.int32, (8, AW), 0)
    place = jnp.where(row < 5, r * 2 + row, r * 2 + row - 8)
    return jnp.where((place >= 0) & (place < 512), lanes_inside(right, 8), 0.0)


def ring_step(x, k, m, hu, hv):
    n = pltpu.roll(x, 1, 0)
    s = pltpu.roll(x, 7, 0)
    w = pltpu.roll(x, 1, 1)
    e = pltpu.roll(x, AW - 1, 1)
    return m * (x + k * (n + s + w + e - 4.0 * x) - hu * (e - w) - hv * (s - n))


def spread_matrix():
    i = lax.broadcasted_iota(jnp.int32, (128, 512), 0)
    j = lax.broadcasted_iota(jnp.int32, (128, 512), 1)
    return jnp.where(j // 4 == i, 1.0, 0.0).astype(BF16)


def two_parts(x):
    high = x.astype(BF16)
    low = (x - high.astype(F32)).astype(BF16)
    return jnp.concatenate([high, low], axis=0)


def spread_columns(rain, right):
    blocks = jnp.concatenate([rain[:, 128 * b : 128 * b + 128] for b in range(7)], axis=0)
    wide = jnp.dot(two_parts(blocks), spread_matrix(), preferred_element_type=F32)
    wide = wide[0:56] + wide[56:112]
    parts = [wide[8 * b : 8 * b + 8] for b in range(6)]
    last = wide[48:56]
    parts.append(jnp.where(right, last[:, 384:512], last[:, 0:128]))
    return jnp.concatenate(parts, axis=1)


def spread_rows(wide):
    row = lax.broadcasted_iota(jnp.int32, (8, TW), 0)
    own = jnp.where(row < 4, wide[0:1, :], wide[1:2, :])
    halo = jnp.where(row < 4, wide[2:3, :], wide[7:8, :])
    return jnp.concatenate([own, halo], axis=0)


def soil_mean(soil, right):
    zero = jnp.zeros((8, 384), F32)
    last = soil[:, TC:TW]
    last = jnp.where(
        right,
        jnp.concatenate([zero, last], axis=1),
        jnp.concatenate([last, zero], axis=1),
    )
    blocks = jnp.concatenate([soil[:, 512 * b : 512 * b + 512] for b in range(6)] + [last], axis=0)
    sums = lax.dot_general(
        two_parts(blocks),
        spread_matrix(),
        (((1,), (1,)), ((), ())),
        preferred_element_type=F32,
    )
    sums = sums[0:56] + sums[56:112]
    wide = jnp.concatenate([sums[8 * b : 8 * b + 8] for b in range(7)], axis=1)
    wide = wide + pltpu.roll(wide, 7, 0)
    wide = wide + pltpu.roll(wide, 6, 0)
    row = lax.broadcasted_iota(jnp.int32, (8, AW), 0)
    return jnp.where(row == 0, wide[0:1, :], jnp.where(row == 1, wide[4:5, :], 0.0)) * 0.0625


def lateral_of(depth, cells):
    row = lax.broadcasted_iota(jnp.int32, (8, 128), 0) * (TC // 128)
    out = []
    for h in range(2):
        cell = cells[h : h + 1, :]
        lane = jnp.broadcast_to(cell % 128, (8, 128))
        block = jnp.broadcast_to(cell // 128, (8, 128)) - row
        total = jnp.zeros((8, 128), F32)
        for b in range(TC // 128):
            got = jnp.take_along_axis(depth[:, 128 * b : 128 * b + 128], lane, axis=1)
            total = jnp.where(block == b, got, total)
        out.append(0.1 * jnp.sum(total, axis=0, keepdims=True))
    return jnp.concatenate(out, axis=1)


def hydro(coef, rq, ring, land, soil, cells, lat):
    for t in range(HSTEPS):
        d = ring[...]
        lat[t : t + 1, :] = lateral_of(ring[0:8, 0:TC], cells)
        soil[...] = soil[...] + 0.05 * land[...] * d[0:8] - 0.02 * soil[...]
        new = rq[...] + coef[0] * d
        new = new + coef[1] * pltpu.roll(d, 1, 1)
        new = new + coef[2] * pltpu.roll(d, TW - 1, 1)
        new = new + coef[3] * pltpu.roll(d, 1, 0)
        new = new + coef[4] * pltpu.roll(d, 15, 0)
        ring[...] = new


def rain_of(q):
    rain = 0.05 * q * q
    return rain, q - rain


def send_edges(odd, ring, q, t, msg_in, msg_out):
    top = ring[0:4, :]
    low = ring[4:8, :]
    for msg in (msg_in, msg_out):
        msg[4:8, :] = jnp.zeros((4, TW), F32)
        msg[4:5, 0:AW] = q[0:1]
        msg[4:5, AW : 2 * AW] = q[1:2]
        msg[4:5, 2 * AW : 3 * AW] = t[0:1]
        msg[5:6, 0:AW] = t[1:2]
    msg_in[0:4, :] = jnp.where(odd, top, low)
    msg_out[0:4, :] = jnp.where(odd, low, top)


def first_body(
    info, u, v, cells, own_msg, elev, cond, rf, mask, code, depth, soil0,
    pin, out, far, own_strip, pair_strip, out_strip, far_strip,
    coef, rain_w, static_w, land, ring, soil, lat, q_out, t_out, k_out, msg_in, msg_out,
    grid, rq, q8, t8, k8,
):
    odd = info[0] == 1
    right = info[1] == 1
    r = info[2]
    hu_t, hv_t = 0.5 * u[0], 0.5 * v[0]
    mine = land_strip(own_strip, right)
    pair = land_strip(pair_strip, right)
    beyond = land_strip(out_strip, right)
    north_strip = jnp.where(odd, pair, beyond)
    south_strip = jnp.where(odd, beyond, pair)
    grid[...] = jnp.zeros_like(grid)
    for a, (ref, off, n, block) in enumerate(
        (
            (elev, 0, 4, 0),
            (cond, 12, 3, 1),
            (rf, 15, 3, 2),
            (mask, 18, 3, 3),
            (code, 4, 4, 4),
            (depth, 8, 4, 5),
        )
    ):
        grid[a, 0:8, 0:TC] = ref[...].astype(F32)
        grid[a, 0:8, TC:TW] = mine[8 * block : 8 * block + 8]
        e_in = pin[off : off + n, :]
        e_out = out[off : off + n, :]
        grid[a, 8 : 8 + n, 0:TC] = jnp.where(odd, e_out, e_in)
        grid[a, 16 - n : 16, 0:TC] = jnp.where(odd, e_in, e_out)
        grid[a, 8 : 8 + n, TC:TW] = south_strip[8 * block : 8 * block + n]
        grid[a, 16 - n : 16, TC:TW] = north_strip[8 * block + 8 - n : 8 * block + 8]
    land[...] = grid[3, 0:8, :]
    soil[:, 0:TC] = soil0[...]
    soil[:, TC:TW] = mine[48:56]
    m = grid[3]
    eta = grid[0]
    lap = (
        pltpu.roll(eta, 1, 1)
        + pltpu.roll(eta, TW - 1, 1)
        + pltpu.roll(eta, 1, 0)
        + pltpu.roll(eta, 15, 0)
        - 4.0 * eta
    )
    mc = m * grid[1]
    codes = grid[4]
    share = 0.2 * m
    coef[0] = 0.75 * m - 4.0 * mc
    coef[1] = mc + jnp.where(pltpu.roll(codes, 1, 1) == 0.0, share, 0.0)
    coef[2] = mc + jnp.where(pltpu.roll(codes, TW - 1, 1) == 2.0, share, 0.0)
    coef[3] = mc + jnp.where(pltpu.roll(codes, 1, 0) == 3.0, share, 0.0)
    coef[4] = mc + jnp.where(pltpu.roll(codes, 15, 0) == 1.0, share, 0.0)
    rain_w[...] = m * grid[2]
    static_w[...] = mc * lap
    ring[...] = grid[5]
    air_mine = air_strip(own_strip, right)
    air_pair = air_strip(pair_strip, right)
    air_out = air_strip(out_strip, right)
    air_far = air_strip(far_strip, right)
    out2_strip = out_strip[24:48, :]
    air_out2 = air_strip(out2_strip, right)
    air_north = jnp.where(odd, air_pair, air_out)
    air_south = jnp.where(odd, air_out, air_pair)
    third_north = jnp.where(odd, air_far, air_out2)
    third_south = jnp.where(odd, air_out2, air_far)
    north = jnp.where(odd, pin[16:24, :], out[16:24, :])
    south = jnp.where(odd, out[16:24, :], pin[16:24, :])
    for ref in (q8, t8, k8):
        ref[...] = jnp.zeros_like(ref)
    for i in range(2):
        for place, msg, strip, cols in (
            (i, own_msg[16:24, :], air_mine, mine),
            (2 + i, south, air_south, south_strip),
            (6 + i, north, air_north, north_strip),
        ):
            q8[place : place + 1, 0:AC] = msg[5:6, i * AC : (i + 1) * AC]
            t8[place : place + 1, 0:AC] = msg[5:6, (2 + i) * AC : (3 + i) * AC]
            k8[place : place + 1, 0:AC] = msg[6:7, i * AC : (i + 1) * AC]
            q8[place : place + 1, AC:AW] = strip[i * FL + Q0 : i * FL + Q0 + 1]
            t8[place : place + 1, AC:AW] = strip[i * FL : i * FL + 1]
            k8[place : place + 1, AC:AW] = cols[56 + i : 57 + i]
    beyond_q = out[22:23, 2 * AC : 3 * AC]
    far_q = jnp.where(odd, far[21:22, AC : 2 * AC], far[21:22, 0:AC])
    q8[4:5, 0:AC] = jnp.where(odd, beyond_q, far_q)
    q8[5:6, 0:AC] = jnp.where(odd, far_q, beyond_q)
    q8[4:5, AC:AW] = third_south[Q0 : Q0 + 1]
    q8[5:6, AC:AW] = third_north[FL + Q0 : FL + Q0 + 1]
    m8 = ring_mask(r, right)
    k = k8[...]
    k_out[...] = k
    q, t = q8[...], t8[...]
    for _ in range(ASTEPS):
        q = ring_step(q, k, m8, hu_t, hv_t)
        t = ring_step(t, k, m8, hu_t, hv_t)
    rain, q = rain_of(q)
    rq[...] = static_w[...] + rain_w[...] * spread_rows(spread_columns(rain, right))
    hydro(coef, rq, ring, land, soil, cells[...], lat)
    coarse = soil_mean(soil[...], right)
    q = q + 0.1 * coarse * jax.nn.sigmoid(t)
    q_out[...] = q
    t_out[...] = t
    send_edges(odd, ring, q, t, msg_in, msg_out)


def second_body(
    info, u, v, cells, coef, rain_w, static_w, land, ring0, soil0, q0, t0, k0, pin, out, far,
    depth_out, coarse_out, q_out, lat,
    ring, soil, rq, q8, t8,
):
    odd = info[0] == 1
    right = info[1] == 1
    r = info[2]
    hu_t, hv_t = 0.5 * u[0], 0.5 * v[0]
    ring[0:8, :] = ring0[0:8, :]
    ring[8:12, :] = jnp.where(odd, out[0:4, :], pin[0:4, :])
    ring[12:16, :] = jnp.where(odd, pin[0:4, :], out[0:4, :])
    soil[...] = soil0[...]
    north = jnp.where(odd, pin[...], out[...])
    south = jnp.where(odd, out[...], pin[...])
    t8[...] = jnp.zeros_like(t8)
    q8[0:2, :] = q0[0:2, :]
    t8[0:2, :] = t0[0:2, :]
    for place, msg in ((2, south), (6, north)):
        q8[place : place + 1, :] = msg[4:5, 0:AW]
        q8[place + 1 : place + 2, :] = msg[4:5, AW : 2 * AW]
        t8[place : place + 1, :] = msg[4:5, 2 * AW : 3 * AW]
        t8[place + 1 : place + 2, :] = msg[5:6, 0:AW]
    beyond_q = out[5:6, AW : 2 * AW]
    far_q = jnp.where(odd, far[4:5, AW : 2 * AW], far[4:5, 0:AW])
    q8[4:5, :] = jnp.where(odd, beyond_q, far_q)
    q8[5:6, :] = jnp.where(odd, far_q, beyond_q)
    m8 = ring_mask(r, right)
    k = k0[...]
    q, t = q8[...], t8[...]
    for _ in range(ASTEPS):
        q = ring_step(q, k, m8, hu_t, hv_t)
        t = ring_step(t, k, m8, hu_t, hv_t)
    rain, q = rain_of(q)
    rq[...] = static_w[...] + rain_w[...] * spread_rows(spread_columns(rain, right))
    hydro(coef, rq, ring, land, soil, cells[...], lat)
    coarse = soil_mean(soil[...], right)
    q = q + 0.1 * coarse * jax.nn.sigmoid(t)
    depth_out[...] = ring[0:8, 0:TC]
    coarse_out[...] = coarse[0:2, 0:AC]
    q_out[...] = q[0:2, 0:AC]


def air_body(
    info, u, v, own, pin, out, far, k8, kfar, own_strip, pair_strip, out_strip, far_strip, qf,
    air_out,
    strips,
):
    odd = info[0] == 1
    right = info[1] == 1
    r = info[2]
    for i, (ref, lo) in enumerate(
        ((own_strip, 0), (pair_strip, 0), (out_strip, 0), (out_strip, 24), (far_strip, 0))
    ):
        strips[i] = air_strip(ref[lo : lo + 24, :], right)
    lanes = lanes_inside(right, 1)
    masks = {}
    for row in range(-3, 5):
        place = r * 2 + row
        inside = jnp.where((place >= 0) & (place < 512), 1.0, 0.0)
        masks[row] = lanes * inside
    kd = {row: k8[row % 8 : row % 8 + 1, :] for row in (-2, -1, 0, 1, 2, 3)}
    kd[-3] = kfar[0:1, :]
    kd[4] = kfar[1:2, :]
    kd = {row: kd[row] * masks[row] for row in kd}

    def group(g, carry):
        at = pl.ds(pl.multiple_of(g * 8, 8), 8)

        def whole(main, strip, i):
            return jnp.concatenate(
                [main, strips[strip, pl.ds(pl.multiple_of(g * 8 + i * FL, 8), 8), :]], axis=1
            )

        x = {0: whole(own[0, at, :], 0, 0), 1: whole(own[1, at, :], 0, 1)}
        p = [whole(pin[i, at, :], 1, i) for i in range(2)]
        o = [whole(out[i, at, :], 2, i) for i in range(2)]
        o2 = [whole(out[2 + i, at, :], 3, i) for i in range(2)]
        f = [whole(far[i, at, :], 4, i) for i in range(2)]
        for i in range(2):
            x[2 + i] = jnp.where(odd, o[i], p[i])
            x[4 + i] = jnp.where(odd, o2[i], f[i])
            x[-2 + i] = jnp.where(odd, p[i], o[i])
            x[-4 + i] = jnp.where(odd, f[i], o2[i])
        hu = 0.5 * u[at, 0:1]
        hv = 0.5 * v[at, 0:1]
        for step in range(ASTEPS * COUPLE):
            new = {}
            for row in range(-3 + step, 5 - step):
                c, n, s = x[row], x[row - 1], x[row + 1]
                w = pltpu.roll(c, 1, 1)
                e = pltpu.roll(c, AW - 1, 1)
                new[row] = (
                    masks[row] * (c - hu * (e - w) - hv * (s - n))
                    + kd[row] * (n + s + w + e - 4.0 * c)
                )
            x = new
        for i in range(2):
            air_out[at, i, :] = x[i][:, 0:AC]
        return carry

    lax.fori_loop(0, FL // 8, group, 0)
    for i in range(2):
        air_out[Q0 : Q0 + 1, i, :] = qf[i : i + 1, :]


def route_body(info, own, got, flow_out, hot):
    j = info[3]
    target = lax.broadcasted_iota(jnp.int32, (2 * LINKS, LINKS), 0).astype(F32)

    def slot(k):
        if k == 0:
            return own[...]
        return got[lax.rem(j - k + 16, 16)]

    data = [slot(k) for k in range(STEPS + 1)]
    flow = [d[8:9, :] for d in data]
    for k in range(STEPS + 1):
        hot[k] = jnp.where(target == data[k][9:10, :], 1.0, 0.0).astype(BF16)
    for t in range(STEPS):
        routed = []
        for k in range(STEPS - t + 1):
            f = flow[k]
            f1 = f.astype(BF16)
            rest = f - f1.astype(F32)
            f2 = rest.astype(BF16)
            f3 = (rest - f2.astype(F32)).astype(BF16)
            lhs = jnp.concatenate([f1, f2, f3, jnp.zeros((13, LINKS), BF16)], axis=0)
            first = 0 if k < STEPS - t else LINKS
            last = 2 * LINKS if k > 0 else LINKS
            y = lax.dot_general(
                lhs,
                hot[k, first:last, :],
                (((1,), (1,)), ((), ())),
                preferred_element_type=F32,
            )
            y = y[0:1] + y[1:2] + y[2:3]
            local = None if first else y[:, 0:LINKS]
            down = y[:, LINKS - first :] if last > LINKS else None
            routed.append((local, down))
        new = []
        for k in range(STEPS - t):
            arrived = routed[k][0] + routed[k + 1][1]
            new.append(flow[k] + 0.5 * (arrived - flow[k]) + data[k][t : t + 1, :])
        flow = new
    flow_out[...] = flow[0]


def shards(
    air, kdiff, u_wind, v_wind, elev, cond, rain_factor, land_mask, flow_code,
    depth_init, soil_init, link_cell, link_down, link_flow,
):
    gx = lax.axis_index("gx")
    row = lax.axis_index("grp") * 16 + gx
    odd = gx % 2
    info = jnp.stack([odd, lax.axis_index("gy"), row, gx]).astype(jnp.int32)
    end = ((gx == 0) | (gx == 15)).astype(F32)
    cells = link_cell.reshape(2, 128)
    ulev = jnp.broadcast_to(jnp.tile(u_wind, 2)[:, None], (FL, 128))
    vlev = jnp.broadcast_to(jnp.tile(v_wind, 2)[:, None], (FL, 128))

    airc, msg_in, msg_out, strip = call(
        pack_body,
        [(2, FL, AC), (32, TC), (24, TC), (24, 128)],
        [info],
        [air.reshape(FL, 2, AC), kdiff, elev, cond, rain_factor, land_mask, flow_code, depth_init, soil_init],
    )
    pin = pair_swap(msg_in)
    pair_strip = jnp.concatenate([pin[24:32, 128 * b : 128 * b + 128] for b in range(3)], axis=0)
    near = near_swap(jnp.concatenate([strip, pair_strip], axis=0))
    nearest = jnp.where(
        odd == 1,
        jnp.concatenate([pin[21, AC : 2 * AC], pin[22, AC : 2 * AC]]),
        jnp.concatenate([pin[21, 0:AC], pin[22, 0:AC]]),
    )
    msg_out = msg_out.at[22, 2 * AC :].set(nearest)
    out = chip_swap(msg_out)
    across = gy_swap(jnp.concatenate([strip, pair_strip, near], axis=0))
    out_strip = jnp.where(end > 0, near, across[48:96])
    far = pair_swap(out)
    far_strip = pair_swap(out_strip)
    own_strip = across[0:24]
    pair_strip = across[24:48]

    air_pair = pair_swap(airc)
    air_near = chip_swap(jnp.concatenate([airc, air_pair], axis=0))
    air_far = pair_swap(air_near[0:2])

    wide = (16, TW)
    (coef, rain_w, static_w, land, ring, soil, lat_a, q, t, k8, msg_in, msg_out) = call(
        first_body,
        [(5, 16, TW), wide, wide, (8, TW), wide, (8, TW), (HSTEPS, LINKS), (8, AW), (8, AW), (8, AW), (8, TW), (8, TW)],
        [info, u_wind, v_wind],
        [cells, msg_out, elev, cond, rain_factor, land_mask, flow_code, depth_init, soil_init, pin, out, far,
         own_strip, pair_strip, out_strip, far_strip],
        [(6, 16, TW), wide, (8, AW), (8, AW), (8, AW)],
    )
    kfar_out = out[22, 3 * AC :]
    kfar_far = jnp.where(odd == 1, far[22, AC : 2 * AC], far[22, 0:AC])
    pinb = pair_swap(msg_in)
    nearest = jnp.where(odd == 1, pinb[4, AW : 2 * AW], pinb[4, 0:AW])
    outb = chip_swap(msg_out.at[5, AW : 2 * AW].set(nearest))
    farb = pair_swap(outb)
    depth, coarse, qf, lat_b = call(
        second_body,
        [(TR, TC), (2, AC), (2, AC), (HSTEPS, LINKS)],
        [info, u_wind, v_wind],
        [cells, coef, rain_w, static_w, land, ring, soil, q, t, k8, pinb, outb, farb],
        [wide, (8, TW), wide, (8, AW), (8, AW)],
    )

    own = jnp.concatenate(
        [lat_a, lat_b, link_flow[None], link_down.astype(F32)[None], jnp.zeros((6, LINKS), F32)]
    )
    before = grp_shift(own)
    later = (jnp.arange(16) > gx)[:, None, None]
    got = lax.all_to_all(jnp.where(later, own[None], before[None]), "gx", 0, 0)

    kn = jnp.where(odd == 1, kfar_far, kfar_out)
    ks = jnp.where(odd == 1, kfar_out, kfar_far)
    kfar = kfar_rows(kn, ks, out_strip, far_strip, odd, lax.axis_index("gy"))
    (air_new,) = call(
        air_body,
        [(FL, 2, AC)],
        [info],
        [ulev, vlev, airc, air_pair, air_near, air_far, k8, kfar, own_strip, pair_strip, out_strip, far_strip, qf],
        [(5, 128, 128)],
    )
    (flow,) = route_call(info, own, got)
    return (air_new.reshape(2, 32, 2, AC), depth, coarse, flow.reshape(LINKS))


def kfar_rows(kn, ks, out_strip, far_strip, odd, gy):
    strip_n = jnp.where(odd == 1, far_strip[0:16, 57], out_strip[24:40, 57])
    strip_s = jnp.where(odd == 1, out_strip[24:40, 56], far_strip[0:16, 56])
    zero = jnp.zeros((112,), F32)

    def place(s):
        return jnp.where(gy == 1, jnp.concatenate([zero, s]), jnp.concatenate([s, zero]))

    return jnp.stack([jnp.concatenate([kn, place(strip_n)]), jnp.concatenate([ks, place(strip_s)])])


def route_call(info, own, got):
    return pl.pallas_call(
        route_body,
        out_shape=[jax.ShapeDtypeStruct((1, LINKS), F32)],
        in_specs=[smem(), vmem(), vmem()],
        out_specs=[vmem()],
        scratch_shapes=[pltpu.VMEM((STEPS + 1, 2 * LINKS, LINKS), BF16)],
        compiler_params=PARAMS,
    )(info, own, got)


def solution(mesh):
    placed = (
        P(None, None, ("grp", "gx"), "gy"),
        P(("grp", "gx"), "gy"),
        P(),
        P(),
        P(("grp", "gx"), "gy"),
        P(("grp", "gx"), "gy"),
        P(("grp", "gx"), "gy"),
        P(("grp", "gx"), "gy"),
        P(("grp", "gx"), "gy"),
        P(("grp", "gx"), "gy"),
        P(("grp", "gx"), "gy"),
        P(AXES),
        P(AXES),
        P(AXES),
    )
    return jax.shard_map(
        shards,
        mesh=mesh,
        in_specs=placed,
        out_specs=(
            P(None, None, ("grp", "gx"), "gy"),
            P(("grp", "gx"), "gy"),
            P(("grp", "gx"), "gy"),
            P(AXES),
        ),
        check_vma=False,
    )
```

```python
import jax
import jax.numpy as jnp
from jax import lax
from jax.experimental import pallas as pl
from jax.experimental.pallas import tpu as pltpu
from jax.sharding import PartitionSpec as P

ASTEPS = 2
HSTEPS = 4
COUPLE = 2
STEPS = HSTEPS * COUPLE

F32 = jnp.float32
BF16 = jnp.bfloat16
AXES = ("grp", "gx", "gy")
ROOM = 16 * 1024 * 1024
WHOLE = 60 * 1024 * 1024

LINKS = 256
TR = 8
TC = 3072
TW = TC + 128
AC = 768
AW = AC + 128
FL = 64
Q0 = 32


def exchange(value, partner):
    pairs = []
    for r in range(256):
        for g in range(2):
            t, h = partner(r, g)
            if 0 <= t < 256:
                pairs.append((r * 2 + g, t * 2 + h))
    return lax.ppermute(value, AXES, pairs)


def outer(r):
    return r + 1 if r % 2 else r - 1


def pair_swap(value):
    return exchange(value, lambda r, g: (r ^ 1, g))


def chip_swap(value):
    return exchange(value, lambda r, g: (outer(r), g))


def near_swap(value):
    return exchange(
        value, lambda r, g: (outer(r), g if outer(r) // 16 == r // 16 else 1 - g)
    )


def gy_swap(value):
    return exchange(value, lambda r, g: (r, 1 - g))


def grp_shift(value):
    return exchange(value, lambda r, g: (r + 16, g))


def vmem():
    return pl.BlockSpec(memory_space=pltpu.VMEM)


def smem():
    return pl.BlockSpec(memory_space=pltpu.SMEM)


def hbm():
    return pl.BlockSpec(memory_space=pltpu.HBM)


def call(body, outs, scalars, arrays, scratch=(), limit=ROOM, far=0):
    space = hbm() if far else vmem()
    return pl.pallas_call(
        body,
        out_shape=[jax.ShapeDtypeStruct(o, F32) for o in outs],
        in_specs=[smem()] * len(scalars) + [space] * len(arrays),
        out_specs=[hbm() if i < far else vmem() for i in range(len(outs))],
        scratch_shapes=[pltpu.VMEM(x, F32) if isinstance(x, tuple) else x for x in scratch],
        compiler_params=pltpu.CompilerParams(vmem_limit_bytes=limit),
    )(*scalars, *arrays)


BLOCK, EDGE = 104, 88
ELEV, COND, RAIN, MASK, CODE, DEPTH, SOIL = range(7)
EDGES = ((ELEV, 0, 4), (COND, 12, 3), (RAIN, 15, 3), (MASK, 18, 3), (CODE, 4, 4), (DEPTH, 8, 4))


def pack_body(
    info, air, kd, elev, cond, rf, mask, code, depth, soil,
    block_h,
    air_v, kd_v, elev_v, cond_v, rf_v, mask_v, code_v, depth_v, soil_v,
    block, sems, sent,
):
    right = info[1] == 1
    near = (kd_v, elev_v, cond_v, rf_v, mask_v, code_v, depth_v, soil_v, air_v)
    copies = [
        pltpu.make_async_copy(src, dst, sems.at[i])
        for i, (src, dst) in enumerate(
            zip((kd, elev, cond, rf, mask, code, depth, soil, air), near)
        )
    ]
    for c in copies:
        c.start()
    block[56:72, :] = jnp.zeros((16, TC), F32)
    for c in copies:
        c.wait()
    for i, ref in enumerate((elev_v, cond_v, rf_v, mask_v, code_v, depth_v, soil_v)):
        block[8 * i : 8 * i + 8, :] = ref[...].astype(F32)
    ends = []
    for r in range(2):
        rows = air_v[:, r, :]
        for h in range(2):
            at = slice((2 * h + r) * AC, (2 * h + r + 1) * AC)
            block[72:104, at] = rows[32 * h : 32 * h + 32, :]
        block[56:57, r * AC : (r + 1) * AC] = rows[Q0 : Q0 + 1, :]
        block[56:57, (2 + r) * AC : (3 + r) * AC] = rows[0:1, :]
        block[57:58, r * AC : (r + 1) * AC] = kd_v[r : r + 1, :]
        ends.append(jnp.where(right, rows[:, 0:128], rows[:, AC - 128 : AC]))
    land = jnp.where(right, block[0:56, 0:128], block[0:56, TC - 128 : TC])
    kblock = jnp.where(right, kd_v[:, 0:128], kd_v[:, AC - 128 : AC])
    square = jnp.concatenate([land, kblock, jnp.zeros((70, 128), F32)], axis=0).T
    strip = jnp.where(right, square[0:16], square[112:128])
    block[64:72, 0:128] = strip[0:8]
    block[64:72, 128:256] = strip[8:16]
    ablock = jnp.concatenate(ends, axis=0).T
    block[64:72, 256:384] = jnp.where(right, ablock[0:8], ablock[120:128])
    result = pltpu.make_async_copy(block, block_h, sent)
    result.start()
    result.wait()


def edge_body(info, block, pin, out, strips):
    odd = info[0] == 1
    for i, off, n in EDGES:
        top = block[8 * i : 8 * i + n, :]
        low = block[8 * i + 8 - n : 8 * i + 8, :]
        out[off : off + n, :] = jnp.where(odd, low, top)
    out[21:23, :] = block[56:58, :]
    out[23:24, :] = jnp.zeros((1, TC), F32)
    for i in range(2):
        a = pin[56 + i : 57 + i, AC : 2 * AC]
        b = pin[56 + i : 57 + i, 0:AC]
        out[22:23, (2 + i) * AC : (3 + i) * AC] = jnp.where(odd, a, b)
        lo, half = 24 + 32 * i, slice(2 * i * AC, 2 * (i + 1) * AC)
        out[lo : lo + 32, 0 : 2 * AC] = block[72:104, half]
        out[lo : lo + 32, 2 * AC : TC] = pin[72:104, half]
    lane = lax.broadcasted_iota(jnp.int32, (8, 128), 1)
    for b in range(2):
        at = slice(b * 128, (b + 1) * 128)
        pair = pltpu.roll(pin[64:72, at], 64, 1)
        strips[8 * b : 8 * b + 8, :] = jnp.where(lane < 64, block[64:72, at], pair)
    strips[16:24, :] = block[64:72, 256:384]
    strips[24:32, :] = pin[64:72, 256:384]


def both_body(strips, near, out):
    out[0:32, :] = strips[...]
    out[32:64, :] = near[...]


def pick_body(info, near, across, out):
    end = (info[3] == 0) | (info[3] == 15)
    out[...] = jnp.where(end, near[...], across[32:64, :])


def chunks_body(info, own, before, out):
    for i in range(16):
        out[i] = jnp.where(info[3] < i, own[...], before[...])


def land_strip(strip, right):
    zero = jnp.zeros((112, 128), F32)
    s = strip[0:16, :]
    return jnp.where(
        right, jnp.concatenate([zero, s], axis=0), jnp.concatenate([s, zero], axis=0)
    ).T


def air_strip(strip, right, lo):
    zero = jnp.zeros((120, 128), F32)
    s = strip[lo : lo + 8, :]
    return jnp.where(
        right, jnp.concatenate([zero, s], axis=0), jnp.concatenate([s, zero], axis=0)
    ).T


def lanes_inside(right, rows):
    lane = lax.broadcasted_iota(jnp.int32, (rows, AW), 1)
    edge = jnp.where(right, AW - 8, AC)
    halo = (lane >= edge) & (lane < edge + 8)
    return jnp.where((lane < AC) | halo, 1.0, 0.0).astype(F32)


def ring_mask(info, right):
    row = lax.broadcasted_iota(jnp.int32, (16, AW), 0)
    place = (info[2] - info[0]) * 2 + jnp.where(row < 8, row, row - 16)
    return jnp.where((place >= 0) & (place < 512), lanes_inside(right, 16), 0.0)


def ring_step(x, k, m, hu, hv):
    n = pltpu.roll(x, 1, 0)
    s = pltpu.roll(x, 15, 0)
    w = pltpu.roll(x, 1, 1)
    e = pltpu.roll(x, AW - 1, 1)
    return m * (x + k * (n + s + w + e - 4.0 * x) - hu * (e - w) - hv * (s - n))


def spread_matrix():
    i = lax.broadcasted_iota(jnp.int32, (128, 512), 0)
    j = lax.broadcasted_iota(jnp.int32, (128, 512), 1)
    return jnp.where(j // 4 == i, 1.0, 0.0).astype(BF16)


def two_parts(x):
    high = x.astype(BF16)
    low = (x - high.astype(F32)).astype(BF16)
    return jnp.concatenate([high, low], axis=0)


def spread_columns(rain, right):
    blocks = jnp.concatenate([rain[:, 128 * b : 128 * b + 128] for b in range(7)], axis=0)
    wide = jnp.dot(two_parts(blocks), spread_matrix(), preferred_element_type=F32)
    wide = wide[0:112] + wide[112:224]
    parts = [wide[16 * b : 16 * b + 16] for b in range(6)]
    last = wide[96:112]
    parts.append(jnp.where(right, last[:, 384:512], last[:, 0:128]))
    return jnp.concatenate(parts, axis=1)


def spread_rows(wide):
    row = lax.broadcasted_iota(jnp.int32, (8, TW), 0)
    return jnp.concatenate(
        [
            jnp.where(row < 4, wide[a : a + 1, :], wide[b : b + 1, :])
            for a, b in ((0, 1), (2, 3), (4, 15))
        ],
        axis=0,
    )


def soil_mean(soil, right):
    zero = jnp.zeros((16, 384), F32)
    last = soil[:, TC:TW]
    last = jnp.where(
        right,
        jnp.concatenate([zero, last], axis=1),
        jnp.concatenate([last, zero], axis=1),
    )
    blocks = jnp.concatenate([soil[:, 512 * b : 512 * b + 512] for b in range(6)] + [last], axis=0)
    sums = lax.dot_general(
        two_parts(blocks),
        spread_matrix(),
        (((1,), (1,)), ((), ())),
        preferred_element_type=F32,
    )
    sums = sums[0:112] + sums[112:224]
    wide = jnp.concatenate([sums[16 * b : 16 * b + 16] for b in range(7)], axis=1)
    wide = wide + pltpu.roll(wide, 15, 0)
    wide = wide + pltpu.roll(wide, 14, 0)
    row = lax.broadcasted_iota(jnp.int32, (16, AW), 0)
    mean = jnp.zeros((16, AW), F32)
    for i in range(4):
        mean = jnp.where(row == i, wide[4 * i : 4 * i + 1, :], mean)
    return mean * 0.0625


def lateral_of(depth, cells):
    row = lax.broadcasted_iota(jnp.int32, (8, 128), 0) * (TC // 128)
    out = []
    for h in range(2):
        cell = cells[h : h + 1, :]
        lane = jnp.broadcast_to(cell % 128, (8, 128))
        block = jnp.broadcast_to(cell // 128, (8, 128)) - row
        total = jnp.zeros((8, 128), F32)
        for b in range(TC // 128):
            got = jnp.take_along_axis(depth[:, 128 * b : 128 * b + 128], lane, axis=1)
            total = jnp.where(block == b, got, total)
        out.append(0.1 * jnp.sum(total, axis=0, keepdims=True))
    return out


def hydro(odd, coef, rq, ring, land, soil, cells, lat, base):
    for t in range(HSTEPS):
        d = ring[...]
        halves = lateral_of(jnp.where(odd, ring[8:16, 0:TC], ring[0:8, 0:TC]), cells)
        for h in range(2):
            lat[base + 2 * t + h : base + 2 * t + h + 1, :] = halves[h]
        soil[...] = soil[...] + 0.05 * land[...] * d[0:16] - 0.02 * soil[...]
        new = rq[...] + coef[0] * d
        new = new + coef[1] * pltpu.roll(d, 1, 1)
        new = new + coef[2] * pltpu.roll(d, TW - 1, 1)
        new = new + coef[3] * pltpu.roll(d, 1, 0)
        new = new + coef[4] * pltpu.roll(d, 23, 0)
        ring[...] = new


def rain_of(q):
    rain = 0.05 * q * q
    return rain, q - rain


def first_body(
    info, u, v, cells, block, pin, out, far, sp, nr, fs,
    coef, rain_w, static_w, land, ring, soil, lat, q_out, t_out, k_out, edge,
    grid, rq,
):
    odd = info[0] == 1
    right = info[1] == 1
    hu_t, hv_t = 0.5 * u[0], 0.5 * v[0]
    square = land_strip(sp, right)
    mine, pair = square[0:64], square[64:128]
    cols = (jnp.where(odd, pair, mine), jnp.where(odd, mine, pair))
    square = land_strip(nr, right)
    beyond, out2 = square[0:64], square[64:128]
    square = land_strip(fs, right)
    other, far2 = square[0:64], square[64:128]
    cols_s, cols_n = jnp.where(odd, beyond, other), jnp.where(odd, other, beyond)
    grid[...] = jnp.zeros_like(grid)

    def chip_rows(ref, i, lo):
        at = slice(8 * i, 8 * i + 8)
        ref[lo : lo + 8, 0:TC] = jnp.where(odd, pin[at, :], block[at, :])
        ref[lo + 8 : lo + 16, 0:TC] = jnp.where(odd, block[at, :], pin[at, :])
        ref[lo : lo + 8, TC:TW] = cols[0][at]
        ref[lo + 8 : lo + 16, TC:TW] = cols[1][at]

    for i, off, n in EDGES:
        chip_rows(grid, i, 24 * i)
        e_out = out[off : off + n, :]
        e_far = far[off : off + n, :]
        lo = 24 * i
        grid[lo + 16 : lo + 16 + n, 0:TC] = jnp.where(odd, e_out, e_far)
        grid[lo + 24 - n : lo + 24, 0:TC] = jnp.where(odd, e_far, e_out)
        grid[lo + 16 : lo + 16 + n, TC:TW] = cols_s[8 * i : 8 * i + n]
        grid[lo + 24 - n : lo + 24, TC:TW] = cols_n[8 * i + 8 - n : 8 * i + 8]
    chip_rows(soil, SOIL, 0)

    def field(i):
        return grid[24 * i : 24 * i + 24, :]

    m = field(MASK)
    land[...] = m[0:16]
    eta = field(ELEV)
    lap = (
        pltpu.roll(eta, 1, 1)
        + pltpu.roll(eta, TW - 1, 1)
        + pltpu.roll(eta, 1, 0)
        + pltpu.roll(eta, 23, 0)
        - 4.0 * eta
    )
    mc = m * field(COND)
    codes = field(CODE)
    share = 0.2 * m
    coef[0] = 0.75 * m - 4.0 * mc
    coef[1] = mc + jnp.where(pltpu.roll(codes, 1, 1) == 0.0, share, 0.0)
    coef[2] = mc + jnp.where(pltpu.roll(codes, TW - 1, 1) == 2.0, share, 0.0)
    coef[3] = mc + jnp.where(pltpu.roll(codes, 1, 0) == 3.0, share, 0.0)
    coef[4] = mc + jnp.where(pltpu.roll(codes, 23, 0) == 1.0, share, 0.0)
    rain_w[...] = m * field(RAIN)
    static_w[...] = mc * lap
    ring[...] = field(DEPTH)
    mine_a, pair_a = air_strip(sp, right, 16), air_strip(sp, right, 24)
    out_a, out2_a = air_strip(nr, right, 16), air_strip(nr, right, 24)
    far_a, far2_a = air_strip(fs, right, 16), air_strip(fs, right, 24)
    own_r, pair_r = block[56:64, :], pin[56:64, :]
    out_r, far_r = out[16:24, :], far[16:24, :]
    for ref in (q_out, t_out, k_out):
        ref[...] = jnp.zeros_like(ref)
    for odd_side, msg, first, air_s, col_s in (
        (None, jnp.where(odd, pair_r, own_r), 0, jnp.where(odd, pair_a, mine_a), cols[0]),
        (None, jnp.where(odd, own_r, pair_r), 2, jnp.where(odd, mine_a, pair_a), cols[1]),
        (False, jnp.where(odd, out_r, far_r), 4, jnp.where(odd, out_a, far_a), cols_s),
        (True, jnp.where(odd, far_r, out_r), 14, jnp.where(odd, far_a, out_a), cols_n),
    ):
        top = 0 if odd_side is None else 5
        for i in range(2):
            at = slice(first + i, first + i + 1)
            q_out[at, 0:AC] = msg[top : top + 1, i * AC : (i + 1) * AC]
            t_out[at, 0:AC] = msg[top : top + 1, (2 + i) * AC : (3 + i) * AC]
            k_out[at, 0:AC] = msg[top + 1 : top + 2, i * AC : (i + 1) * AC]
            q_out[at, AC:AW] = air_s[i * FL + Q0 : i * FL + Q0 + 1]
            t_out[at, AC:AW] = air_s[i * FL : i * FL + 1]
            k_out[at, AC:AW] = col_s[56 + i : 57 + i]
        if odd_side is not None:
            place = 13 if odd_side else 6
            i = 1 if odd_side else 0
            at = slice(place, place + 1)
            third_a = jnp.where(odd, far2_a, out2_a) if odd_side else jnp.where(odd, out2_a, far2_a)
            third = jnp.where(odd, far2, out2) if odd_side else jnp.where(odd, out2, far2)
            q_out[at, 0:AC] = msg[6:7, 2 * AC : 3 * AC]
            k_out[at, 0:AC] = msg[6:7, 3 * AC : 4 * AC]
            q_out[at, AC:AW] = third_a[i * FL + Q0 : i * FL + Q0 + 1]
            k_out[at, AC:AW] = third[56 + i : 57 + i]
    m8 = ring_mask(info, right)
    k = k_out[...]
    q, t = q_out[...], t_out[...]
    for _ in range(ASTEPS):
        q = ring_step(q, k, m8, hu_t, hv_t)
        t = ring_step(t, k, m8, hu_t, hv_t)
    rain, q = rain_of(q)
    rq[...] = static_w[...] + rain_w[...] * spread_rows(spread_columns(rain, right))
    lat[...] = jnp.zeros_like(lat)
    hydro(odd, coef, rq, ring, land, soil, cells[...], lat, 0)
    q = q + 0.1 * soil_mean(soil[...], right) * jax.nn.sigmoid(t)
    q_out[...] = q
    t_out[...] = t
    edge[0:4, :] = jnp.where(odd, ring[12:16, :], ring[0:4, :])
    edge[4:8, :] = jnp.zeros((4, TW), F32)
    for lane, a, b in ((0, 2, 0), (1, 3, 1), (2, 1, 2)):
        at = slice(lane * AW, (lane + 1) * AW)
        edge[4:5, at] = jnp.where(odd, q[a : a + 1], q[b : b + 1])
        if lane < 2:
            edge[5:6, at] = jnp.where(odd, t[a : a + 1], t[b : b + 1])


def second_body(
    info, u, v, cells, link_flow, link_down, coef, rain_w, static_w, land, ring0, soil0, lat0,
    q0, t0, k0, out, far,
    depth_out, coarse_out, q_out, lat,
    ring, soil, rq, q8, t8,
):
    odd = info[0] == 1
    right = info[1] == 1
    hu_t, hv_t = 0.5 * u[0], 0.5 * v[0]
    ring[0:16, :] = ring0[0:16, :]
    south = jnp.where(odd, out[...], far[...])
    north = jnp.where(odd, far[...], out[...])
    ring[16:20, :] = south[0:4]
    ring[20:24, :] = north[0:4]
    soil[...] = soil0[...]
    q8[...] = jnp.zeros_like(q8)
    t8[...] = jnp.zeros_like(t8)
    q8[0:4, :] = q0[0:4, :]
    t8[0:4, :] = t0[0:4, :]
    for places, msg in (((4, 5, 6), south), ((14, 15, 13), north)):
        for i, place in enumerate(places):
            q8[place : place + 1, :] = msg[4:5, i * AW : (i + 1) * AW]
            if i < 2:
                t8[place : place + 1, :] = msg[5:6, i * AW : (i + 1) * AW]
    m8 = ring_mask(info, right)
    k = k0[...]
    q, t = q8[...], t8[...]
    for _ in range(ASTEPS):
        q = ring_step(q, k, m8, hu_t, hv_t)
        t = ring_step(t, k, m8, hu_t, hv_t)
    rain, q = rain_of(q)
    rq[...] = static_w[...] + rain_w[...] * spread_rows(spread_columns(rain, right))
    lat[0:8, :] = lat0[...]
    lat[16:24, :] = jnp.zeros((8, 128), F32)
    lat[16:18, :] = link_flow[...]
    lat[18:20, :] = link_down[...].astype(F32)
    hydro(odd, coef, rq, ring, land, soil, cells[...], lat, 8)
    coarse = soil_mean(soil[...], right)
    q = q + 0.1 * coarse * jax.nn.sigmoid(t)
    depth_out[...] = jnp.where(odd, ring[8:16, 0:TC], ring[0:8, 0:TC])
    coarse_out[...] = jnp.where(odd, coarse[2:4, 0:AC], coarse[0:2, 0:AC])
    q_out[...] = jnp.where(odd, q[2:4, 0:AC], q[0:2, 0:AC])


def air_body(
    info, u, v, block, pin, out, far, k16, sp, nr, fs,
    air_out,
    strips,
):
    odd = info[0] == 1
    right = info[1] == 1
    r = info[2]
    for i, (ref, lo) in enumerate(((sp, 16), (sp, 24), (nr, 16), (nr, 24), (fs, 16))):
        strips[i] = air_strip(ref, right, lo)
    lanes = lanes_inside(right, 1)
    masks, kd = {}, {}
    for row in range(-3, 5):
        place = r * 2 + row
        masks[row] = lanes * jnp.where((place >= 0) & (place < 512), 1.0, 0.0)
        a, b = (2 + row) % 16, row % 16
        kd[row] = jnp.where(odd, k16[a : a + 1, :], k16[b : b + 1, :]) * masks[row]

    def group(half, g):
        at = pl.multiple_of(g * 8, 8)
        own8 = pl.ds(72 + at, 8)
        out8 = pl.ds(24 + 32 * half + at, 8)

        def whole(ref, rows, lane, strip, i):
            side = strips[strip, pl.ds(32 * half + i * FL + at, 8), :]
            return jnp.concatenate([ref[rows, lane * AC : (lane + 1) * AC], side], axis=1)

        x = {i: whole(block, own8, 2 * half + i, 0, i) for i in range(2)}
        p = [whole(pin, own8, 2 * half + i, 1, i) for i in range(2)]
        o = [whole(out, out8, i, 2, i) for i in range(2)]
        o2 = [whole(out, out8, 2 + i, 3, i) for i in range(2)]
        f = [whole(far, out8, i, 4, i) for i in range(2)]
        for i in range(2):
            x[2 + i] = jnp.where(odd, o[i], p[i])
            x[4 + i] = jnp.where(odd, o2[i], f[i])
            x[-2 + i] = jnp.where(odd, p[i], o[i])
            x[-4 + i] = jnp.where(odd, f[i], o2[i])
        row8 = lax.broadcasted_iota(jnp.int32, (8, AW), 0)
        hu = jnp.zeros((8, AW), F32)
        hv = jnp.zeros((8, AW), F32)
        for i in range(8):
            hu = jnp.where(row8 == i, 0.5 * u[at + i], hu)
            hv = jnp.where(row8 == i, 0.5 * v[at + i], hv)
        for step in range(ASTEPS * COUPLE):
            new = {}
            for row in range(-3 + step, 5 - step):
                c, n, s = x[row], x[row - 1], x[row + 1]
                w = pltpu.roll(c, 1, 1)
                e = pltpu.roll(c, AW - 1, 1)
                new[row] = (
                    masks[row] * (c - hu * (e - w) - hv * (s - n))
                    + kd[row] * (n + s + w + e - 4.0 * c)
                )
            x = new
        for i in range(2):
            air_out[pl.ds(32 * half + at, 8), i, :] = x[i][:, 0:AC]

    for half in range(2):
        lax.fori_loop(0, 4, lambda g, c, half=half: (group(half, g), c)[1], 0)


def route_body(info, own, got, flow_out, hot):
    j = info[3]
    target = lax.broadcasted_iota(jnp.int32, (2 * LINKS, LINKS), 0).astype(F32)
    data = [own[...]] + [got[lax.rem(j - k + 16, 16)] for k in range(1, STEPS + 1)]

    def wide(d, i):
        return jnp.concatenate([d[2 * i : 2 * i + 1, :], d[2 * i + 1 : 2 * i + 2, :]], axis=1)

    flow = [wide(d, 8) for d in data]
    for k in range(STEPS + 1):
        hot[k] = jnp.where(target == wide(data[k], 9), 1.0, 0.0).astype(BF16)
    for t in range(STEPS):
        routed = []
        for k in range(STEPS - t + 1):
            f = flow[k]
            f1 = f.astype(BF16)
            rest = f - f1.astype(F32)
            f2 = rest.astype(BF16)
            f3 = (rest - f2.astype(F32)).astype(BF16)
            lhs = jnp.concatenate([f1, f2, f3, jnp.zeros((13, LINKS), BF16)], axis=0)
            first = 0 if k < STEPS - t else LINKS
            last = 2 * LINKS if k > 0 else LINKS
            y = lax.dot_general(
                lhs,
                hot[k, first:last, :],
                (((1,), (1,)), ((), ())),
                preferred_element_type=F32,
            )
            y = y[0:1] + y[1:2] + y[2:3]
            local = None if first else y[:, 0:LINKS]
            down = y[:, LINKS - first :] if last > LINKS else None
            routed.append((local, down))
        new = []
        for k in range(STEPS - t):
            arrived = routed[k][0] + routed[k + 1][1]
            new.append(flow[k] + 0.5 * (arrived - flow[k]) + wide(data[k], t))
        flow = new
    flow_out[...] = flow[0]


def shards(
    air, kdiff, u_wind, v_wind, elev, cond, rain_factor, land_mask, flow_code,
    depth_init, soil_init, link_cell, link_down, link_flow,
):
    gx = lax.axis_index("gx")
    odd = gx % 2
    row = lax.axis_index("grp") * 16 + gx
    info = jnp.stack([odd, lax.axis_index("gy"), row, gx]).astype(jnp.int32)
    pairs = link_cell.reshape(2, 128), link_flow.reshape(2, 128), link_down.reshape(2, 128)

    land_v = pltpu.VMEM((TR, TC), F32)
    code_v = pltpu.VMEM((TR, TC), jnp.int32)
    (block,) = call(
        pack_body,
        [(BLOCK, TC)],
        [info],
        [air.reshape(FL, 2, AC), kdiff, elev, cond, rain_factor, land_mask, flow_code, depth_init, soil_init],
        [(FL, 2, AC), (2, AC), land_v, land_v, land_v, code_v, code_v, land_v, land_v, (BLOCK, TC),
         pltpu.SemaphoreType.DMA((9,)), pltpu.SemaphoreType.DMA],
        limit=WHOLE,
        far=1,
    )
    pin = pair_swap(block)
    edge, strips = call(edge_body, [(EDGE, TC), (32, 128)], [info], [block, pin])
    near = near_swap(strips)
    out = chip_swap(edge)
    (both,) = call(both_body, [(64, 128)], [], [strips, near])
    sp = gy_swap(both)
    (nr,) = call(pick_body, [(32, 128)], [info], [near, sp])
    ready, _ = lax.optimization_barrier((out, sp))
    far = pair_swap(ready)
    fs = pair_swap(nr)

    wide, chip, flat = (24, TW), (16, TW), (16, AW)
    (coef, rain_w, static_w, land, ring, soil, lat, q, t, k16, edge) = call(
        first_body,
        [(5, 24, TW), wide, wide, chip, wide, chip, (8, 128), flat, flat, flat, (8, TW)],
        [info, u_wind, v_wind],
        [pairs[0], block, pin, out, far, sp, nr, fs],
        [(144, TW), wide],
    )
    outb = chip_swap(edge)
    farb = pair_swap(outb)
    depth, coarse, qf, own = call(
        second_body,
        [(TR, TC), (2, AC), (2, AC), (24, 128)],
        [info, u_wind, v_wind],
        [*pairs, coef, rain_w, static_w, land, ring, soil, lat, q, t, k16, outb, farb],
        [wide, chip, wide, flat, flat],
    )
    before = grp_shift(own)
    (chunks,) = call(chunks_body, [(16, 24, 128)], [info], [own, before])
    got = lax.all_to_all(chunks, "gx", 0, 0)
    (air_new,) = call(
        air_body,
        [(FL, 2, AC)],
        [info, u_wind, v_wind],
        [block, pin, out, far, k16, sp, nr, fs],
        [(5, 128, 128)],
    )
    air_new = air_new.at[Q0].set(qf)

    got, air_new = lax.optimization_barrier((got, air_new))
    (flow,) = call(
        route_body,
        [(1, LINKS)],
        [info],
        [own, got],
        [pltpu.VMEM((STEPS + 1, 2 * LINKS, LINKS), BF16)],
    )
    return (air_new.reshape(2, 32, 2, AC), depth, coarse, flow.reshape(LINKS))


def solution(mesh):
    placed = (
        P(None, None, ("grp", "gx"), "gy"),
        P(("grp", "gx"), "gy"),
        P(),
        P(),
        P(("grp", "gx"), "gy"),
        P(("grp", "gx"), "gy"),
        P(("grp", "gx"), "gy"),
        P(("grp", "gx"), "gy"),
        P(("grp", "gx"), "gy"),
        P(("grp", "gx"), "gy"),
        P(("grp", "gx"), "gy"),
        P(AXES),
        P(AXES),
        P(AXES),
    )
    return jax.shard_map(
        shards,
        mesh=mesh,
        in_specs=placed,
        out_specs=(
            P(None, None, ("grp", "gx"), "gy"),
            P(("grp", "gx"), "gy"),
            P(("grp", "gx"), "gy"),
            P(AXES),
        ),
        check_vma=False,
    )
```

```python
import jax
import jax.numpy as jnp
from jax import lax
from jax.experimental import pallas as pl
from jax.experimental.pallas import tpu as pltpu
from jax.sharding import PartitionSpec as P

ASTEPS = 2
HSTEPS = 4
COUPLE = 2
STEPS = HSTEPS * COUPLE

F32 = jnp.float32
BF16 = jnp.bfloat16
AXES = ("grp", "gx", "gy")
ROOM = 16 * 1024 * 1024
WHOLE = 60 * 1024 * 1024

LINKS = 256
TR = 8
TC = 3072
TW = TC + 128
AC = 768
AW = AC + 128
FL = 64
Q0 = 32


def exchange(value, partner):
    pairs = []
    for r in range(256):
        for g in range(2):
            t, h = partner(r, g)
            if 0 <= t < 256:
                pairs.append((r * 2 + g, t * 2 + h))
    return lax.ppermute(value, AXES, pairs)


def outer(r):
    return r + 1 if r % 2 else r - 1


def pair_swap(value):
    return exchange(value, lambda r, g: (r ^ 1, g))


def chip_swap(value):
    return exchange(value, lambda r, g: (outer(r), g))


def near_swap(value):
    return exchange(
        value, lambda r, g: (outer(r), g if outer(r) // 16 == r // 16 else 1 - g)
    )


def gy_swap(value):
    return exchange(value, lambda r, g: (r, 1 - g))


def grp_shift(value):
    return exchange(value, lambda r, g: (r + 16, g))


def vmem():
    return pl.BlockSpec(memory_space=pltpu.VMEM)


def smem():
    return pl.BlockSpec(memory_space=pltpu.SMEM)


def hbm():
    return pl.BlockSpec(memory_space=pltpu.HBM)


def call(body, outs, scalars, arrays, scratch=(), limit=ROOM, far=0):
    space = hbm() if far else vmem()
    return pl.pallas_call(
        body,
        out_shape=[jax.ShapeDtypeStruct(o, F32) for o in outs],
        in_specs=[smem()] * len(scalars) + [space] * len(arrays),
        out_specs=[hbm() if i < far else vmem() for i in range(len(outs))],
        scratch_shapes=[pltpu.VMEM(x, F32) if isinstance(x, tuple) else x for x in scratch],
        compiler_params=pltpu.CompilerParams(vmem_limit_bytes=limit),
    )(*scalars, *arrays)


BLOCK, EDGE = 104, 56
ELEV, COND, RAIN, MASK, CODE, DEPTH, SOIL = range(7)
EDGES = ((ELEV, 0, 4), (COND, 12, 3), (RAIN, 15, 3), (MASK, 18, 3), (CODE, 4, 4), (DEPTH, 8, 4))


def pack_body(
    info, air, kd, elev, cond, rf, mask, code, depth, soil, links,
    block_h,
    links_v, air_v, kd_v, elev_v, cond_v, rf_v, mask_v, code_v, depth_v, soil_v,
    block, sems, sent,
):
    right = info[1] == 1
    near = (kd_v, elev_v, cond_v, rf_v, mask_v, code_v, depth_v, soil_v, air_v, links_v)
    copies = [
        pltpu.make_async_copy(src, dst, sems.at[i])
        for i, (src, dst) in enumerate(
            zip((kd, elev, cond, rf, mask, code, depth, soil, air, links), near)
        )
    ]
    for c in copies:
        c.start()
    block[56:72, :] = jnp.zeros((16, TC), F32)
    for c in copies:
        c.wait()
    for i, ref in enumerate((elev_v, cond_v, rf_v, mask_v, code_v, depth_v, soil_v)):
        block[8 * i : 8 * i + 8, :] = ref[...].astype(F32)
    block[58:59, 0:LINKS] = links_v[...]
    ends = []
    for r in range(2):
        rows = air_v[:, r, :]
        for h in range(2):
            at = slice((2 * h + r) * AC, (2 * h + r + 1) * AC)
            block[72:104, at] = rows[32 * h : 32 * h + 32, :]
        block[56:57, r * AC : (r + 1) * AC] = rows[Q0 : Q0 + 1, :]
        block[56:57, (2 + r) * AC : (3 + r) * AC] = rows[0:1, :]
        block[57:58, r * AC : (r + 1) * AC] = kd_v[r : r + 1, :]
        ends.append(jnp.where(right, rows[:, 0:128], rows[:, AC - 128 : AC]))
    land = jnp.where(right, block[0:56, 0:128], block[0:56, TC - 128 : TC])
    kblock = jnp.where(right, kd_v[:, 0:128], kd_v[:, AC - 128 : AC])
    square = jnp.concatenate([land, kblock, jnp.zeros((70, 128), F32)], axis=0).T
    strip = jnp.where(right, square[0:16], square[112:128])
    block[64:72, 0:128] = strip[0:8]
    block[64:72, 128:256] = strip[8:16]
    ablock = jnp.concatenate(ends, axis=0).T
    block[64:72, 256:384] = jnp.where(right, ablock[0:8], ablock[120:128])
    result = pltpu.make_async_copy(block, block_h, sent)
    result.start()
    result.wait()


def edge_body(info, block, pin, out, strips):
    odd = info[0] == 1
    for i, off, n in EDGES:
        top = block[8 * i : 8 * i + n, :]
        low = block[8 * i + 8 - n : 8 * i + 8, :]
        out[off : off + n, :] = jnp.where(odd, low, top)
    out[21:24, :] = block[56:59, :]
    for i in range(2):
        a = pin[56 + i : 57 + i, AC : 2 * AC]
        b = pin[56 + i : 57 + i, 0:AC]
        out[22:23, (2 + i) * AC : (3 + i) * AC] = jnp.where(odd, a, b)
    out[24:56, :] = block[72:104, :]
    lane = lax.broadcasted_iota(jnp.int32, (8, 128), 1)
    for b in range(2):
        at = slice(b * 128, (b + 1) * 128)
        pair = pltpu.roll(pin[64:72, at], 64, 1)
        strips[8 * b : 8 * b + 8, :] = jnp.where(lane < 64, block[64:72, at], pair)
    strips[16:24, :] = block[64:72, 256:384]
    strips[24:32, :] = pin[64:72, 256:384]


def pair_air_body(edge, pin, out):
    out[...] = pin[72:104, :]


def both_body(strips, near, out):
    out[0:32, :] = strips[...]
    out[32:64, :] = near[...]


def pick_body(info, near, across, out):
    end = (info[3] == 0) | (info[3] == 15)
    out[...] = jnp.where(end, near[...], across[32:64, :])


def chunks_body(info, own, before, out):
    for i in range(16):
        src = jnp.where(info[3] < i, own[...], before[...])
        out[i, 0:12, :] = src[0:12]
        out[i, 12:14, :] = jnp.where(info[3] == (i + 15) % 16, src[12:14], src[16:18])
        out[i, 14:16, :] = src[18:20]


def land_strip(strip, right):
    zero = jnp.zeros((112, 128), F32)
    s = strip[0:16, :]
    return jnp.where(
        right, jnp.concatenate([zero, s], axis=0), jnp.concatenate([s, zero], axis=0)
    ).T


def air_strip(strip, right, lo):
    zero = jnp.zeros((120, 128), F32)
    s = strip[lo : lo + 8, :]
    return jnp.where(
        right, jnp.concatenate([zero, s], axis=0), jnp.concatenate([s, zero], axis=0)
    ).T


def lanes_inside(right, rows):
    lane = lax.broadcasted_iota(jnp.int32, (rows, AW), 1)
    edge = jnp.where(right, AW - 8, AC)
    halo = (lane >= edge) & (lane < edge + 8)
    return jnp.where((lane < AC) | halo, 1.0, 0.0).astype(F32)


def ring_mask(info, right):
    row = lax.broadcasted_iota(jnp.int32, (16, AW), 0)
    place = (info[2] - info[0]) * 2 + jnp.where(row < 8, row, row - 16)
    return jnp.where((place >= 0) & (place < 512), lanes_inside(right, 16), 0.0)


def ring_step(x, k, m, hu, hv):
    n = pltpu.roll(x, 1, 0)
    s = pltpu.roll(x, 15, 0)
    w = pltpu.roll(x, 1, 1)
    e = pltpu.roll(x, AW - 1, 1)
    return m * (x + k * (n + s + w + e - 4.0 * x) - hu * (e - w) - hv * (s - n))


def spread_matrix():
    i = lax.broadcasted_iota(jnp.int32, (128, 512), 0)
    j = lax.broadcasted_iota(jnp.int32, (128, 512), 1)
    return jnp.where(j // 4 == i, 1.0, 0.0).astype(BF16)


def two_parts(x):
    high = x.astype(BF16)
    low = (x - high.astype(F32)).astype(BF16)
    return jnp.concatenate([high, low], axis=0)


def spread_columns(rain, right):
    blocks = jnp.concatenate([rain[:, 128 * b : 128 * b + 128] for b in range(7)], axis=0)
    wide = jnp.dot(two_parts(blocks), spread_matrix(), preferred_element_type=F32)
    wide = wide[0:112] + wide[112:224]
    parts = [wide[16 * b : 16 * b + 16] for b in range(6)]
    last = wide[96:112]
    parts.append(jnp.where(right, last[:, 384:512], last[:, 0:128]))
    return jnp.concatenate(parts, axis=1)


def spread_rows(wide):
    row = lax.broadcasted_iota(jnp.int32, (8, TW), 0)
    return jnp.concatenate(
        [
            jnp.where(row < 4, wide[a : a + 1, :], wide[b : b + 1, :])
            for a, b in ((0, 1), (2, 3), (4, 15))
        ],
        axis=0,
    )


def soil_mean(soil, right):
    zero = jnp.zeros((16, 384), F32)
    last = soil[:, TC:TW]
    last = jnp.where(
        right,
        jnp.concatenate([zero, last], axis=1),
        jnp.concatenate([last, zero], axis=1),
    )
    blocks = jnp.concatenate([soil[:, 512 * b : 512 * b + 512] for b in range(6)] + [last], axis=0)
    sums = lax.dot_general(
        two_parts(blocks),
        spread_matrix(),
        (((1,), (1,)), ((), ())),
        preferred_element_type=F32,
    )
    sums = sums[0:112] + sums[112:224]
    wide = jnp.concatenate([sums[16 * b : 16 * b + 16] for b in range(7)], axis=1)
    wide = wide + pltpu.roll(wide, 15, 0)
    wide = wide + pltpu.roll(wide, 14, 0)
    row = lax.broadcasted_iota(jnp.int32, (16, AW), 0)
    mean = jnp.zeros((16, AW), F32)
    for i in range(4):
        mean = jnp.where(row == i, wide[4 * i : 4 * i + 1, :], mean)
    return mean * 0.0625


def lateral_of(depth, cells):
    row = lax.broadcasted_iota(jnp.int32, (8, 128), 0) * (TC // 128)
    out = []
    for h in range(2):
        cell = cells[h : h + 1, :]
        lane = jnp.broadcast_to(cell % 128, (8, 128))
        block = jnp.broadcast_to(cell // 128, (8, 128)) - row
        total = jnp.zeros((8, 128), F32)
        for b in range(TC // 128):
            got = jnp.take_along_axis(depth[:, 128 * b : 128 * b + 128], lane, axis=1)
            total = jnp.where(block == b, got, total)
        out.append(0.1 * jnp.sum(total, axis=0, keepdims=True))
    return out


def hydro(odd, coef, rq, ring, land, soil, cells, lat, base):
    for t in range(HSTEPS):
        d = ring[...]
        halves = lateral_of(jnp.where(odd, ring[8:16, 0:TC], ring[0:8, 0:TC]), cells)
        for h in range(2):
            lat[base + 2 * t + h : base + 2 * t + h + 1, :] = halves[h]
        soil[...] = soil[...] + 0.05 * land[...] * d[0:16] - 0.02 * soil[...]
        new = rq[...] + coef[0] * d
        new = new + coef[1] * pltpu.roll(d, 1, 1)
        new = new + coef[2] * pltpu.roll(d, TW - 1, 1)
        new = new + coef[3] * pltpu.roll(d, 1, 0)
        new = new + coef[4] * pltpu.roll(d, 23, 0)
        ring[...] = new


def rain_of(q):
    rain = 0.05 * q * q
    return rain, q - rain


def first_body(
    info, u, v, cells, block, pin, out, far, sp, nr, fs,
    coef, rain_w, static_w, land, ring, soil, lat, q_out, t_out, k_out, edge, above,
    grid, rq,
):
    odd = info[0] == 1
    right = info[1] == 1
    hu_t, hv_t = 0.5 * u[0], 0.5 * v[0]
    square = land_strip(sp, right)
    mine, pair = square[0:64], square[64:128]
    cols = (jnp.where(odd, pair, mine), jnp.where(odd, mine, pair))
    square = land_strip(nr, right)
    beyond, out2 = square[0:64], square[64:128]
    square = land_strip(fs, right)
    other, far2 = square[0:64], square[64:128]
    cols_s, cols_n = jnp.where(odd, beyond, other), jnp.where(odd, other, beyond)
    grid[...] = jnp.zeros_like(grid)

    def chip_rows(ref, i, lo):
        at = slice(8 * i, 8 * i + 8)
        ref[lo : lo + 8, 0:TC] = jnp.where(odd, pin[at, :], block[at, :])
        ref[lo + 8 : lo + 16, 0:TC] = jnp.where(odd, block[at, :], pin[at, :])
        ref[lo : lo + 8, TC:TW] = cols[0][at]
        ref[lo + 8 : lo + 16, TC:TW] = cols[1][at]

    for i, off, n in EDGES:
        chip_rows(grid, i, 24 * i)
        e_out = out[off : off + n, :]
        e_far = far[off : off + n, :]
        lo = 24 * i
        grid[lo + 16 : lo + 16 + n, 0:TC] = jnp.where(odd, e_out, e_far)
        grid[lo + 24 - n : lo + 24, 0:TC] = jnp.where(odd, e_far, e_out)
        grid[lo + 16 : lo + 16 + n, TC:TW] = cols_s[8 * i : 8 * i + n]
        grid[lo + 24 - n : lo + 24, TC:TW] = cols_n[8 * i + 8 - n : 8 * i + 8]
    chip_rows(soil, SOIL, 0)

    def field(i):
        return grid[24 * i : 24 * i + 24, :]

    m = field(MASK)
    land[...] = m[0:16]
    eta = field(ELEV)
    lap = (
        pltpu.roll(eta, 1, 1)
        + pltpu.roll(eta, TW - 1, 1)
        + pltpu.roll(eta, 1, 0)
        + pltpu.roll(eta, 23, 0)
        - 4.0 * eta
    )
    mc = m * field(COND)
    codes = field(CODE)
    share = 0.2 * m
    coef[0] = 0.75 * m - 4.0 * mc
    coef[1] = mc + jnp.where(pltpu.roll(codes, 1, 1) == 0.0, share, 0.0)
    coef[2] = mc + jnp.where(pltpu.roll(codes, TW - 1, 1) == 2.0, share, 0.0)
    coef[3] = mc + jnp.where(pltpu.roll(codes, 1, 0) == 3.0, share, 0.0)
    coef[4] = mc + jnp.where(pltpu.roll(codes, 23, 0) == 1.0, share, 0.0)
    rain_w[...] = m * field(RAIN)
    static_w[...] = mc * lap
    ring[...] = field(DEPTH)
    mine_a, pair_a = air_strip(sp, right, 16), air_strip(sp, right, 24)
    out_a, out2_a = air_strip(nr, right, 16), air_strip(nr, right, 24)
    far_a, far2_a = air_strip(fs, right, 16), air_strip(fs, right, 24)
    own_r, pair_r = block[56:64, :], pin[56:64, :]
    out_r, far_r = out[16:24, :], far[16:24, :]
    for ref in (q_out, t_out, k_out):
        ref[...] = jnp.zeros_like(ref)
    for odd_side, msg, first, air_s, col_s in (
        (None, jnp.where(odd, pair_r, own_r), 0, jnp.where(odd, pair_a, mine_a), cols[0]),
        (None, jnp.where(odd, own_r, pair_r), 2, jnp.where(odd, mine_a, pair_a), cols[1]),
        (False, jnp.where(odd, out_r, far_r), 4, jnp.where(odd, out_a, far_a), cols_s),
        (True, jnp.where(odd, far_r, out_r), 14, jnp.where(odd, far_a, out_a), cols_n),
    ):
        top = 0 if odd_side is None else 5
        for i in range(2):
            at = slice(first + i, first + i + 1)
            q_out[at, 0:AC] = msg[top : top + 1, i * AC : (i + 1) * AC]
            t_out[at, 0:AC] = msg[top : top + 1, (2 + i) * AC : (3 + i) * AC]
            k_out[at, 0:AC] = msg[top + 1 : top + 2, i * AC : (i + 1) * AC]
            q_out[at, AC:AW] = air_s[i * FL + Q0 : i * FL + Q0 + 1]
            t_out[at, AC:AW] = air_s[i * FL : i * FL + 1]
            k_out[at, AC:AW] = col_s[56 + i : 57 + i]
        if odd_side is not None:
            place = 13 if odd_side else 6
            i = 1 if odd_side else 0
            at = slice(place, place + 1)
            third_a = jnp.where(odd, far2_a, out2_a) if odd_side else jnp.where(odd, out2_a, far2_a)
            third = jnp.where(odd, far2, out2) if odd_side else jnp.where(odd, out2, far2)
            q_out[at, 0:AC] = msg[6:7, 2 * AC : 3 * AC]
            k_out[at, 0:AC] = msg[6:7, 3 * AC : 4 * AC]
            q_out[at, AC:AW] = third_a[i * FL + Q0 : i * FL + Q0 + 1]
            k_out[at, AC:AW] = third[56 + i : 57 + i]
    m8 = ring_mask(info, right)
    k = k_out[...]
    q, t = q_out[...], t_out[...]
    for _ in range(ASTEPS):
        q = ring_step(q, k, m8, hu_t, hv_t)
        t = ring_step(t, k, m8, hu_t, hv_t)
    for h in range(2):
        at = slice(128 * h, 128 * h + 128)
        above[h : h + 1, :] = jnp.where(odd, pin[58:59, at], out[23:24, at])
    rain, q = rain_of(q)
    rq[...] = static_w[...] + rain_w[...] * spread_rows(spread_columns(rain, right))
    lat[...] = jnp.zeros_like(lat)
    hydro(odd, coef, rq, ring, land, soil, cells[...], lat, 0)
    q = q + 0.1 * soil_mean(soil[...], right) * jax.nn.sigmoid(t)
    q_out[...] = q
    t_out[...] = t
    edge[0:4, :] = jnp.where(odd, ring[12:16, :], ring[0:4, :])
    edge[4:8, :] = jnp.zeros((4, TW), F32)
    for lane, a, b in ((0, 2, 0), (1, 3, 1), (2, 1, 2)):
        at = slice(lane * AW, (lane + 1) * AW)
        edge[4:5, at] = jnp.where(odd, q[a : a + 1], q[b : b + 1])
        if lane < 2:
            edge[5:6, at] = jnp.where(odd, t[a : a + 1], t[b : b + 1])


def second_body(
    info, u, v, cells, link_flow, link_down, coef, rain_w, static_w, land, ring0, soil0, lat0,
    q0, t0, k0, out, far,
    depth_out, coarse_out, q_out, lat,
    ring, soil, rq, q8, t8,
):
    odd = info[0] == 1
    right = info[1] == 1
    hu_t, hv_t = 0.5 * u[0], 0.5 * v[0]
    ring[0:16, :] = ring0[0:16, :]
    south = jnp.where(odd, out[...], far[...])
    north = jnp.where(odd, far[...], out[...])
    ring[16:20, :] = south[0:4]
    ring[20:24, :] = north[0:4]
    soil[...] = soil0[...]
    q8[...] = jnp.zeros_like(q8)
    t8[...] = jnp.zeros_like(t8)
    q8[0:4, :] = q0[0:4, :]
    t8[0:4, :] = t0[0:4, :]
    for places, msg in (((4, 5, 6), south), ((14, 15, 13), north)):
        for i, place in enumerate(places):
            q8[place : place + 1, :] = msg[4:5, i * AW : (i + 1) * AW]
            if i < 2:
                t8[place : place + 1, :] = msg[5:6, i * AW : (i + 1) * AW]
    m8 = ring_mask(info, right)
    k = k0[...]
    q, t = q8[...], t8[...]
    for _ in range(ASTEPS):
        q = ring_step(q, k, m8, hu_t, hv_t)
        t = ring_step(t, k, m8, hu_t, hv_t)
    rain, q = rain_of(q)
    rq[...] = static_w[...] + rain_w[...] * spread_rows(spread_columns(rain, right))
    lat[0:8, :] = lat0[...]
    lat[16:24, :] = jnp.zeros((8, 128), F32)
    lat[16:18, :] = link_flow[...]
    lat[18:20, :] = link_down[...].astype(F32)
    hydro(odd, coef, rq, ring, land, soil, cells[...], lat, 8)
    coarse = soil_mean(soil[...], right)
    q = q + 0.1 * coarse * jax.nn.sigmoid(t)
    depth_out[...] = jnp.where(odd, ring[8:16, 0:TC], ring[0:8, 0:TC])
    coarse_out[...] = jnp.where(odd, coarse[2:4, 0:AC], coarse[0:2, 0:AC])
    q_out[...] = jnp.where(odd, q[2:4, 0:AC], q[0:2, 0:AC])


def air_body(
    info, u, v, block, pin, out, second, far, k16, sp, nr, fs,
    air_out,
    strips,
):
    odd = info[0] == 1
    right = info[1] == 1
    r = info[2]
    for i, (ref, lo) in enumerate(((sp, 16), (sp, 24), (nr, 16), (nr, 24), (fs, 16))):
        strips[i] = air_strip(ref, right, lo)
    lanes = lanes_inside(right, 1)
    masks, kd = {}, {}
    for row in range(-3, 5):
        place = r * 2 + row
        masks[row] = lanes * jnp.where((place >= 0) & (place < 512), 1.0, 0.0)
        a, b = (2 + row) % 16, row % 16
        kd[row] = jnp.where(odd, k16[a : a + 1, :], k16[b : b + 1, :]) * masks[row]

    def group(half, g):
        at = pl.multiple_of(g * 8, 8)
        own8 = pl.ds(72 + at, 8)
        out8 = pl.ds(24 + at, 8)

        def whole(ref, rows, lane, strip, i):
            side = strips[strip, pl.ds(32 * half + i * FL + at, 8), :]
            return jnp.concatenate([ref[rows, lane * AC : (lane + 1) * AC], side], axis=1)

        x = {i: whole(block, own8, 2 * half + i, 0, i) for i in range(2)}
        p = [whole(pin, own8, 2 * half + i, 1, i) for i in range(2)]
        o = [whole(out, out8, 2 * half + i, 2, i) for i in range(2)]
        o2 = [whole(second, pl.ds(at, 8), 2 * half + i, 3, i) for i in range(2)]
        f = [whole(far, out8, 2 * half + i, 4, i) for i in range(2)]
        for i in range(2):
            x[2 + i] = jnp.where(odd, o[i], p[i])
            x[4 + i] = jnp.where(odd, o2[i], f[i])
            x[-2 + i] = jnp.where(odd, p[i], o[i])
            x[-4 + i] = jnp.where(odd, f[i], o2[i])
        row8 = lax.broadcasted_iota(jnp.int32, (8, AW), 0)
        hu = jnp.zeros((8, AW), F32)
        hv = jnp.zeros((8, AW), F32)
        for i in range(8):
            hu = jnp.where(row8 == i, 0.5 * u[at + i], hu)
            hv = jnp.where(row8 == i, 0.5 * v[at + i], hv)
        for step in range(ASTEPS * COUPLE):
            new = {}
            for row in range(-3 + step, 5 - step):
                c, n, s = x[row], x[row - 1], x[row + 1]
                w = pltpu.roll(c, 1, 1)
                e = pltpu.roll(c, AW - 1, 1)
                new[row] = (
                    masks[row] * (c - hu * (e - w) - hv * (s - n))
                    + kd[row] * (n + s + w + e - 4.0 * c)
                )
            x = new
        for i in range(2):
            air_out[pl.ds(32 * half + at, 8), i, :] = x[i][:, 0:AC]

    for half in range(2):
        lax.fori_loop(0, 4, lambda g, c, half=half: (group(half, g), c)[1], 0)


def route_body(info, own, got, above, flow_out, hot):
    j = info[3]
    target = lax.broadcasted_iota(jnp.int32, (2 * LINKS, LINKS), 0).astype(F32)
    data = [own[...]] + [got[lax.rem(j - k + 16, 16)] for k in range(1, STEPS + 1)]

    def wide(d, i):
        return jnp.concatenate([d[2 * i : 2 * i + 1, :], d[2 * i + 1 : 2 * i + 2, :]], axis=1)

    flow = [wide(own[...], 8), wide(above[...], 0)] + [wide(d, 6) for d in data[2:]]
    for k in range(STEPS + 1):
        hot[k] = jnp.where(target == wide(data[k], 7 if k else 9), 1.0, 0.0).astype(BF16)
    for t in range(STEPS):
        routed = []
        for k in range(STEPS - t + 1):
            f = flow[k]
            f1 = f.astype(BF16)
            rest = f - f1.astype(F32)
            f2 = rest.astype(BF16)
            f3 = (rest - f2.astype(F32)).astype(BF16)
            lhs = jnp.concatenate([f1, f2, f3, jnp.zeros((13, LINKS), BF16)], axis=0)
            first = 0 if k < STEPS - t else LINKS
            last = 2 * LINKS if k > 0 else LINKS
            y = lax.dot_general(
                lhs,
                hot[k, first:last, :],
                (((1,), (1,)), ((), ())),
                preferred_element_type=F32,
            )
            y = y[0:1] + y[1:2] + y[2:3]
            local = None if first else y[:, 0:LINKS]
            down = y[:, LINKS - first :] if last > LINKS else None
            routed.append((local, down))
        new = []
        for k in range(STEPS - t):
            arrived = routed[k][0] + routed[k + 1][1]
            new.append(flow[k] + 0.5 * (arrived - flow[k]) + wide(data[k], t))
        flow = new
    flow_out[...] = flow[0]


def shards(
    air, kdiff, u_wind, v_wind, elev, cond, rain_factor, land_mask, flow_code,
    depth_init, soil_init, link_cell, link_down, link_flow,
):
    gx = lax.axis_index("gx")
    odd = gx % 2
    row = lax.axis_index("grp") * 16 + gx
    info = jnp.stack([odd, lax.axis_index("gy"), row, gx]).astype(jnp.int32)
    pairs = link_cell.reshape(2, 128), link_flow.reshape(2, 128), link_down.reshape(2, 128)

    land_v = pltpu.VMEM((TR, TC), F32)
    code_v = pltpu.VMEM((TR, TC), jnp.int32)
    (block,) = call(
        pack_body,
        [(BLOCK, TC)],
        [info],
        [air.reshape(FL, 2, AC), kdiff, elev, cond, rain_factor, land_mask, flow_code, depth_init, soil_init,
         link_flow.reshape(1, LINKS)],
        [(1, LINKS), (FL, 2, AC), (2, AC), land_v, land_v, land_v, code_v, code_v, land_v, land_v, (BLOCK, TC),
         pltpu.SemaphoreType.DMA((10,)), pltpu.SemaphoreType.DMA],
        limit=WHOLE,
        far=1,
    )
    pin = pair_swap(block)
    edge, strips = call(edge_body, [(EDGE, TC), (32, 128)], [info], [block, pin])
    near = near_swap(strips)
    out = chip_swap(edge)
    (both,) = call(both_body, [(64, 128)], [], [strips, near])
    sp = gy_swap(both)
    (nr,) = call(pick_body, [(32, 128)], [info], [near, sp])
    ready, _ = lax.optimization_barrier((out, sp))
    far = pair_swap(ready)
    fs = pair_swap(nr)

    wide, chip, flat = (24, TW), (16, TW), (16, AW)
    (coef, rain_w, static_w, land, ring, soil, lat, q, t, k16, edge, above) = call(
        first_body,
        [(5, 24, TW), wide, wide, chip, wide, chip, (8, 128), flat, flat, flat, (8, TW), (2, 128)],
        [info, u_wind, v_wind],
        [pairs[0], block, pin, out, far, sp, nr, fs],
        [(144, TW), wide],
    )
    outb = chip_swap(edge)
    (second,) = call(pair_air_body, [(32, TC)], [], [edge, pin])
    second = chip_swap(second)
    farb = pair_swap(outb)
    depth, coarse, qf, own = call(
        second_body,
        [(TR, TC), (2, AC), (2, AC), (24, 128)],
        [info, u_wind, v_wind],
        [*pairs, coef, rain_w, static_w, land, ring, soil, lat, q, t, k16, outb, farb],
        [wide, chip, wide, flat, flat],
    )
    before = grp_shift(own)
    (chunks,) = call(chunks_body, [(16, 16, 128)], [info], [own, before])
    got = lax.all_to_all(chunks, "gx", 0, 0)
    (air_new,) = call(
        air_body,
        [(FL, 2, AC)],
        [info, u_wind, v_wind],
        [block, pin, out, second, far, k16, sp, nr, fs],
        [(5, 128, 128)],
    )
    air_new = air_new.at[Q0].set(qf)

    got, air_new = lax.optimization_barrier((got, air_new))
    (flow,) = call(
        route_body,
        [(1, LINKS)],
        [info],
        [own, got, above],
        [pltpu.VMEM((STEPS + 1, 2 * LINKS, LINKS), BF16)],
    )
    return (air_new.reshape(2, 32, 2, AC), depth, coarse, flow.reshape(LINKS))


def solution(mesh):
    placed = (
        P(None, None, ("grp", "gx"), "gy"),
        P(("grp", "gx"), "gy"),
        P(),
        P(),
        P(("grp", "gx"), "gy"),
        P(("grp", "gx"), "gy"),
        P(("grp", "gx"), "gy"),
        P(("grp", "gx"), "gy"),
        P(("grp", "gx"), "gy"),
        P(("grp", "gx"), "gy"),
        P(("grp", "gx"), "gy"),
        P(AXES),
        P(AXES),
        P(AXES),
    )
    return jax.shard_map(
        shards,
        mesh=mesh,
        in_specs=placed,
        out_specs=(
            P(None, None, ("grp", "gx"), "gy"),
            P(("grp", "gx"), "gy"),
            P(("grp", "gx"), "gy"),
            P(AXES),
        ),
        check_vma=False,
    )
```

```python
import jax
import jax.numpy as jnp
from jax import lax
from jax.experimental import pallas as pl
from jax.experimental.pallas import tpu as pltpu
from jax.sharding import PartitionSpec as P

ASTEPS = 2
HSTEPS = 4
COUPLE = 2
STEPS = HSTEPS * COUPLE

F32 = jnp.float32
BF16 = jnp.bfloat16
AXES = ("grp", "gx", "gy")
ROOM = 16 * 1024 * 1024
WHOLE = 60 * 1024 * 1024

LINKS = 256
TR = 8
TC = 3072
TW = TC + 128
AC = 768
AW = AC + 128
FL = 64
Q0 = 32


def exchange(value, partner):
    pairs = []
    for r in range(256):
        for g in range(2):
            t, h = partner(r, g)
            if 0 <= t < 256:
                pairs.append((r * 2 + g, t * 2 + h))
    return lax.ppermute(value, AXES, pairs)


def outer(r):
    return r + 1 if r % 2 else r - 1


def pair_swap(value):
    return exchange(value, lambda r, g: (r ^ 1, g))


def chip_swap(value):
    return exchange(value, lambda r, g: (outer(r), g))


def beside(r, t, g):
    return (t, g if t // 16 == r // 16 else 1 - g)


def near_swap(value):
    return exchange(value, lambda r, g: beside(r, outer(r), g))


def second_shift(value):
    return exchange(value, lambda r, g: beside(r, r - 2 if r % 2 else r + 2, g))


def gy_swap(value):
    return exchange(value, lambda r, g: (r if 0 < r % 16 < 15 else -1, 1 - g))


def grp_shift(value):
    return exchange(value, lambda r, g: (r + 16, g))


def vmem():
    return pl.BlockSpec(memory_space=pltpu.VMEM)


def smem():
    return pl.BlockSpec(memory_space=pltpu.SMEM)


def hbm():
    return pl.BlockSpec(memory_space=pltpu.HBM)


def call(body, outs, scalars, arrays, scratch=(), limit=ROOM, far=0):
    space = hbm() if far else vmem()
    return pl.pallas_call(
        body,
        out_shape=[jax.ShapeDtypeStruct(o, F32) for o in outs],
        in_specs=[smem()] * len(scalars) + [space] * len(arrays),
        out_specs=[hbm() if i < far else vmem() for i in range(len(outs))],
        scratch_shapes=[pltpu.VMEM(x, F32) if isinstance(x, tuple) else x for x in scratch],
        compiler_params=pltpu.CompilerParams(vmem_limit_bytes=limit),
    )(*scalars, *arrays)


BLOCK, EDGE = 104, 56
ELEV, COND, RAIN, MASK, CODE, DEPTH, SOIL = range(7)
EDGES = ((ELEV, 0, 4), (COND, 12, 3), (RAIN, 15, 3), (MASK, 18, 3), (CODE, 4, 4), (DEPTH, 8, 4))


def pack_body(
    info, air, kd, elev, cond, rf, mask, code, depth, soil, links,
    block_h, strip_h,
    links_v, air_v, kd_v, elev_v, cond_v, rf_v, mask_v, code_v, depth_v, soil_v,
    block, strip, sems, sent,
):
    right = info[1] == 1
    near = (kd_v, elev_v, cond_v, rf_v, mask_v, code_v, depth_v, soil_v, air_v, links_v)
    copies = [
        pltpu.make_async_copy(src, dst, sems.at[i])
        for i, (src, dst) in enumerate(
            zip((kd, elev, cond, rf, mask, code, depth, soil, air, links), near)
        )
    ]
    for c in copies:
        c.start()
    block[56:72, :] = jnp.zeros((16, TC), F32)
    for c in copies:
        c.wait()
    for i, ref in enumerate((elev_v, cond_v, rf_v, mask_v, code_v, depth_v, soil_v)):
        block[8 * i : 8 * i + 8, :] = ref[...].astype(F32)
    block[58:59, 0:LINKS] = links_v[...]
    ends = []
    for r in range(2):
        rows = air_v[:, r, :]
        for h in range(2):
            at = slice((2 * h + r) * AC, (2 * h + r + 1) * AC)
            block[72:104, at] = rows[32 * h : 32 * h + 32, :]
        block[56:57, r * AC : (r + 1) * AC] = rows[Q0 : Q0 + 1, :]
        block[56:57, (2 + r) * AC : (3 + r) * AC] = rows[0:1, :]
        block[57:58, r * AC : (r + 1) * AC] = kd_v[r : r + 1, :]
        ends.append(jnp.where(right, rows[:, 0:128], rows[:, AC - 128 : AC]))
    land = jnp.where(right, block[0:56, 0:128], block[0:56, TC - 128 : TC])
    kblock = jnp.where(right, kd_v[:, 0:128], kd_v[:, AC - 128 : AC])
    square = jnp.concatenate([land, kblock, jnp.zeros((70, 128), F32)], axis=0).T
    strip[0:16, :] = jnp.where(right, square[0:16], square[112:128])
    ablock = jnp.concatenate(ends, axis=0).T
    strip[16:24, :] = jnp.where(right, ablock[0:8], ablock[120:128])
    for b in range(3):
        block[64:72, b * 128 : (b + 1) * 128] = strip[8 * b : 8 * b + 8, :]
    results = [
        pltpu.make_async_copy(src, dst, sent.at[i])
        for i, (src, dst) in enumerate(((strip, strip_h), (block, block_h)))
    ]
    for c in results:
        c.start()
    for c in results:
        c.wait()


def edge_body(info, block, pin, near, near2, out, strips, beyond):
    odd = info[0] == 1
    for i, off, n in EDGES:
        top = block[8 * i : 8 * i + n, :]
        low = block[8 * i + 8 - n : 8 * i + 8, :]
        out[off : off + n, :] = jnp.where(odd, low, top)
    out[21:24, :] = block[56:59, :]
    for i in range(2):
        a = pin[56 + i : 57 + i, AC : 2 * AC]
        b = pin[56 + i : 57 + i, 0:AC]
        out[22:23, (2 + i) * AC : (3 + i) * AC] = jnp.where(odd, a, b)
    out[24:56, :] = block[72:104, :]
    lane = lax.broadcasted_iota(jnp.int32, (8, 128), 1)
    for b in range(2):
        at, rows = slice(b * 128, (b + 1) * 128), slice(8 * b, 8 * b + 8)
        pair = pltpu.roll(pin[64:72, at], 64, 1)
        strips[rows, :] = jnp.where(lane < 64, block[64:72, at], pair)
        beyond[rows, :] = jnp.where(lane < 64, near[rows, :], pltpu.roll(near2[rows, :], 64, 1))
    strips[16:24, :] = block[64:72, 256:384]
    strips[24:32, :] = pin[64:72, 256:384]
    beyond[16:24, :] = near[16:24, :]
    beyond[24:32, :] = near2[16:24, :]
    strips[32:64, :] = beyond[...]


def pair_air_body(edge, pin, out):
    out[...] = pin[72:104, :]


def pick_body(info, near, across, out):
    end = (info[3] == 0) | (info[3] == 15)
    out[0:32, :] = across[0:32, :]
    out[32:64, :] = jnp.where(end, near[...], across[32:64, :])


def chunks_body(info, own, before, out):
    for i in range(16):
        src = jnp.where(info[3] < i, own[...], before[...])
        out[i, 0:12, :] = src[0:12]
        out[i, 12:14, :] = jnp.where(info[3] == (i + 15) % 16, src[12:14], src[16:18])
        out[i, 14:16, :] = src[18:20]


def land_strip(strip, right):
    zero = jnp.zeros((112, 128), F32)
    s = strip[0:16, :]
    return jnp.where(
        right, jnp.concatenate([zero, s], axis=0), jnp.concatenate([s, zero], axis=0)
    ).T


def air_strip(strip, right, lo):
    zero = jnp.zeros((120, 128), F32)
    s = strip[lo : lo + 8, :]
    return jnp.where(
        right, jnp.concatenate([zero, s], axis=0), jnp.concatenate([s, zero], axis=0)
    ).T


def lanes_inside(right, rows):
    lane = lax.broadcasted_iota(jnp.int32, (rows, AW), 1)
    edge = jnp.where(right, AW - 8, AC)
    halo = (lane >= edge) & (lane < edge + 8)
    return jnp.where((lane < AC) | halo, 1.0, 0.0).astype(F32)


def ring_mask(info, right):
    row = lax.broadcasted_iota(jnp.int32, (16, AW), 0)
    place = (info[2] - info[0]) * 2 + jnp.where(row < 8, row, row - 16)
    return jnp.where((place >= 0) & (place < 512), lanes_inside(right, 16), 0.0)


def ring_step(x, k, m, hu, hv):
    n = pltpu.roll(x, 1, 0)
    s = pltpu.roll(x, 15, 0)
    w = pltpu.roll(x, 1, 1)
    e = pltpu.roll(x, AW - 1, 1)
    return m * (x + k * (n + s + w + e - 4.0 * x) - hu * (e - w) - hv * (s - n))


def spread_matrix():
    i = lax.broadcasted_iota(jnp.int32, (128, 512), 0)
    j = lax.broadcasted_iota(jnp.int32, (128, 512), 1)
    return jnp.where(j // 4 == i, 1.0, 0.0).astype(BF16)


def two_parts(x):
    high = x.astype(BF16)
    low = (x - high.astype(F32)).astype(BF16)
    return jnp.concatenate([high, low], axis=0)


def spread_columns(rain, right):
    blocks = jnp.concatenate([rain[:, 128 * b : 128 * b + 128] for b in range(7)], axis=0)
    wide = jnp.dot(two_parts(blocks), spread_matrix(), preferred_element_type=F32)
    wide = wide[0:112] + wide[112:224]
    parts = [wide[16 * b : 16 * b + 16] for b in range(6)]
    last = wide[96:112]
    parts.append(jnp.where(right, last[:, 384:512], last[:, 0:128]))
    return jnp.concatenate(parts, axis=1)


def spread_rows(wide):
    row = lax.broadcasted_iota(jnp.int32, (8, TW), 0)
    return jnp.concatenate(
        [
            jnp.where(row < 4, wide[a : a + 1, :], wide[b : b + 1, :])
            for a, b in ((0, 1), (2, 3), (4, 15))
        ],
        axis=0,
    )


def soil_mean(soil, right):
    zero = jnp.zeros((16, 384), F32)
    last = soil[:, TC:TW]
    last = jnp.where(
        right,
        jnp.concatenate([zero, last], axis=1),
        jnp.concatenate([last, zero], axis=1),
    )
    blocks = jnp.concatenate([soil[:, 512 * b : 512 * b + 512] for b in range(6)] + [last], axis=0)
    sums = lax.dot_general(
        two_parts(blocks),
        spread_matrix(),
        (((1,), (1,)), ((), ())),
        preferred_element_type=F32,
    )
    sums = sums[0:112] + sums[112:224]
    wide = jnp.concatenate([sums[16 * b : 16 * b + 16] for b in range(7)], axis=1)
    wide = wide + pltpu.roll(wide, 15, 0)
    wide = wide + pltpu.roll(wide, 14, 0)
    row = lax.broadcasted_iota(jnp.int32, (16, AW), 0)
    mean = jnp.zeros((16, AW), F32)
    for i in range(4):
        mean = jnp.where(row == i, wide[4 * i : 4 * i + 1, :], mean)
    return mean * 0.0625


def lateral_of(depth, cells):
    row = lax.broadcasted_iota(jnp.int32, (8, 128), 0) * (TC // 128)
    out = []
    for h in range(2):
        cell = cells[h : h + 1, :]
        lane = jnp.broadcast_to(cell % 128, (8, 128))
        block = jnp.broadcast_to(cell // 128, (8, 128)) - row
        total = jnp.zeros((8, 128), F32)
        for b in range(TC // 128):
            got = jnp.take_along_axis(depth[:, 128 * b : 128 * b + 128], lane, axis=1)
            total = jnp.where(block == b, got, total)
        out.append(0.1 * jnp.sum(total, axis=0, keepdims=True))
    return out


def hydro(odd, coef, rq, ring, land, soil, cells, lat, base):
    for t in range(HSTEPS):
        d = ring[...]
        halves = lateral_of(jnp.where(odd, ring[8:16, 0:TC], ring[0:8, 0:TC]), cells)
        for h in range(2):
            lat[base + 2 * t + h : base + 2 * t + h + 1, :] = halves[h]
        soil[...] = soil[...] + 0.05 * land[...] * d[0:16] - 0.02 * soil[...]
        new = rq[...] + coef[0] * d
        new = new + coef[1] * pltpu.roll(d, 1, 1)
        new = new + coef[2] * pltpu.roll(d, TW - 1, 1)
        new = new + coef[3] * pltpu.roll(d, 1, 0)
        new = new + coef[4] * pltpu.roll(d, 23, 0)
        ring[...] = new


def rain_of(q):
    rain = 0.05 * q * q
    return rain, q - rain


def first_body(
    info, u, v, cells, block, pin, out, far, strips, far_strips,
    coef, rain_w, static_w, land, ring, soil, lat, q_out, t_out, k_out, edge, above, sp,
    grid, rq,
):
    odd = info[0] == 1
    right = info[1] == 1
    hu_t, hv_t = 0.5 * u[0], 0.5 * v[0]
    end = (info[3] == 0) | (info[3] == 15)
    sp[0:16, :] = jnp.where(end, pltpu.roll(far_strips[0:16, :], 64, 1), strips[0:16, :])
    sp[16:24, :] = jnp.where(end, far_strips[24:32, :], strips[16:24, :])
    sp[24:32, :] = jnp.where(end, far_strips[16:24, :], strips[24:32, :])
    nr, fs = strips.at[32:64, :], far_strips.at[32:64, :]
    square = land_strip(sp, right)
    mine, pair = square[0:64], square[64:128]
    cols = (jnp.where(odd, pair, mine), jnp.where(odd, mine, pair))
    square = land_strip(nr, right)
    beyond, out2 = square[0:64], square[64:128]
    square = land_strip(fs, right)
    other, far2 = square[0:64], square[64:128]
    cols_s, cols_n = jnp.where(odd, beyond, other), jnp.where(odd, other, beyond)
    grid[...] = jnp.zeros_like(grid)

    def chip_rows(ref, i, lo):
        at = slice(8 * i, 8 * i + 8)
        ref[lo : lo + 8, 0:TC] = jnp.where(odd, pin[at, :], block[at, :])
        ref[lo + 8 : lo + 16, 0:TC] = jnp.where(odd, block[at, :], pin[at, :])
        ref[lo : lo + 8, TC:TW] = cols[0][at]
        ref[lo + 8 : lo + 16, TC:TW] = cols[1][at]

    for i, off, n in EDGES:
        chip_rows(grid, i, 24 * i)
        e_out = out[off : off + n, :]
        e_far = far[off : off + n, :]
        lo = 24 * i
        grid[lo + 16 : lo + 16 + n, 0:TC] = jnp.where(odd, e_out, e_far)
        grid[lo + 24 - n : lo + 24, 0:TC] = jnp.where(odd, e_far, e_out)
        grid[lo + 16 : lo + 16 + n, TC:TW] = cols_s[8 * i : 8 * i + n]
        grid[lo + 24 - n : lo + 24, TC:TW] = cols_n[8 * i + 8 - n : 8 * i + 8]
    chip_rows(soil, SOIL, 0)

    def field(i):
        return grid[24 * i : 24 * i + 24, :]

    m = field(MASK)
    land[...] = m[0:16]
    eta = field(ELEV)
    lap = (
        pltpu.roll(eta, 1, 1)
        + pltpu.roll(eta, TW - 1, 1)
        + pltpu.roll(eta, 1, 0)
        + pltpu.roll(eta, 23, 0)
        - 4.0 * eta
    )
    mc = m * field(COND)
    codes = field(CODE)
    share = 0.2 * m
    coef[0] = 0.75 * m - 4.0 * mc
    coef[1] = mc + jnp.where(pltpu.roll(codes, 1, 1) == 0.0, share, 0.0)
    coef[2] = mc + jnp.where(pltpu.roll(codes, TW - 1, 1) == 2.0, share, 0.0)
    coef[3] = mc + jnp.where(pltpu.roll(codes, 1, 0) == 3.0, share, 0.0)
    coef[4] = mc + jnp.where(pltpu.roll(codes, 23, 0) == 1.0, share, 0.0)
    rain_w[...] = m * field(RAIN)
    static_w[...] = mc * lap
    ring[...] = field(DEPTH)
    mine_a, pair_a = air_strip(sp, right, 16), air_strip(sp, right, 24)
    out_a, out2_a = air_strip(nr, right, 16), air_strip(nr, right, 24)
    far_a, far2_a = air_strip(fs, right, 16), air_strip(fs, right, 24)
    own_r, pair_r = block[56:64, :], pin[56:64, :]
    out_r, far_r = out[16:24, :], far[16:24, :]
    for ref in (q_out, t_out, k_out):
        ref[...] = jnp.zeros_like(ref)
    for odd_side, msg, first, air_s, col_s in (
        (None, jnp.where(odd, pair_r, own_r), 0, jnp.where(odd, pair_a, mine_a), cols[0]),
        (None, jnp.where(odd, own_r, pair_r), 2, jnp.where(odd, mine_a, pair_a), cols[1]),
        (False, jnp.where(odd, out_r, far_r), 4, jnp.where(odd, out_a, far_a), cols_s),
        (True, jnp.where(odd, far_r, out_r), 14, jnp.where(odd, far_a, out_a), cols_n),
    ):
        top = 0 if odd_side is None else 5
        for i in range(2):
            at = slice(first + i, first + i + 1)
            q_out[at, 0:AC] = msg[top : top + 1, i * AC : (i + 1) * AC]
            t_out[at, 0:AC] = msg[top : top + 1, (2 + i) * AC : (3 + i) * AC]
            k_out[at, 0:AC] = msg[top + 1 : top + 2, i * AC : (i + 1) * AC]
            q_out[at, AC:AW] = air_s[i * FL + Q0 : i * FL + Q0 + 1]
            t_out[at, AC:AW] = air_s[i * FL : i * FL + 1]
            k_out[at, AC:AW] = col_s[56 + i : 57 + i]
        if odd_side is not None:
            place = 13 if odd_side else 6
            i = 1 if odd_side else 0
            at = slice(place, place + 1)
            third_a = jnp.where(odd, far2_a, out2_a) if odd_side else jnp.where(odd, out2_a, far2_a)
            third = jnp.where(odd, far2, out2) if odd_side else jnp.where(odd, out2, far2)
            q_out[at, 0:AC] = msg[6:7, 2 * AC : 3 * AC]
            k_out[at, 0:AC] = msg[6:7, 3 * AC : 4 * AC]
            q_out[at, AC:AW] = third_a[i * FL + Q0 : i * FL + Q0 + 1]
            k_out[at, AC:AW] = third[56 + i : 57 + i]
    m8 = ring_mask(info, right)
    k = k_out[...]
    q, t = q_out[...], t_out[...]
    for _ in range(ASTEPS):
        q = ring_step(q, k, m8, hu_t, hv_t)
        t = ring_step(t, k, m8, hu_t, hv_t)
    for h in range(2):
        at = slice(128 * h, 128 * h + 128)
        above[h : h + 1, :] = jnp.where(odd, pin[58:59, at], out[23:24, at])
    rain, q = rain_of(q)
    rq[...] = static_w[...] + rain_w[...] * spread_rows(spread_columns(rain, right))
    lat[...] = jnp.zeros_like(lat)
    hydro(odd, coef, rq, ring, land, soil, cells[...], lat, 0)
    q = q + 0.1 * soil_mean(soil[...], right) * jax.nn.sigmoid(t)
    q_out[...] = q
    t_out[...] = t
    edge[0:4, :] = jnp.where(odd, ring[12:16, :], ring[0:4, :])
    edge[4:8, :] = jnp.zeros((4, TW), F32)
    for lane, a, b in ((0, 2, 0), (1, 3, 1), (2, 1, 2)):
        at = slice(lane * AW, (lane + 1) * AW)
        edge[4:5, at] = jnp.where(odd, q[a : a + 1], q[b : b + 1])
        if lane < 2:
            edge[5:6, at] = jnp.where(odd, t[a : a + 1], t[b : b + 1])


def second_body(
    info, u, v, cells, link_flow, link_down, coef, rain_w, static_w, land, ring0, soil0, lat0,
    q0, t0, k0, out, far,
    depth_out, coarse_out, q_out, lat,
    ring, soil, rq, q8, t8,
):
    odd = info[0] == 1
    right = info[1] == 1
    hu_t, hv_t = 0.5 * u[0], 0.5 * v[0]
    ring[0:16, :] = ring0[0:16, :]
    south = jnp.where(odd, out[...], far[...])
    north = jnp.where(odd, far[...], out[...])
    ring[16:20, :] = south[0:4]
    ring[20:24, :] = north[0:4]
    soil[...] = soil0[...]
    q8[...] = jnp.zeros_like(q8)
    t8[...] = jnp.zeros_like(t8)
    q8[0:4, :] = q0[0:4, :]
    t8[0:4, :] = t0[0:4, :]
    for places, msg in (((4, 5, 6), south), ((14, 15, 13), north)):
        for i, place in enumerate(places):
            q8[place : place + 1, :] = msg[4:5, i * AW : (i + 1) * AW]
            if i < 2:
                t8[place : place + 1, :] = msg[5:6, i * AW : (i + 1) * AW]
    m8 = ring_mask(info, right)
    k = k0[...]
    q, t = q8[...], t8[...]
    for _ in range(ASTEPS):
        q = ring_step(q, k, m8, hu_t, hv_t)
        t = ring_step(t, k, m8, hu_t, hv_t)
    rain, q = rain_of(q)
    rq[...] = static_w[...] + rain_w[...] * spread_rows(spread_columns(rain, right))
    lat[0:8, :] = lat0[...]
    lat[16:24, :] = jnp.zeros((8, 128), F32)
    lat[16:18, :] = link_flow[...]
    lat[18:20, :] = link_down[...].astype(F32)
    hydro(odd, coef, rq, ring, land, soil, cells[...], lat, 8)
    coarse = soil_mean(soil[...], right)
    q = q + 0.1 * coarse * jax.nn.sigmoid(t)
    depth_out[...] = jnp.where(odd, ring[8:16, 0:TC], ring[0:8, 0:TC])
    coarse_out[...] = jnp.where(odd, coarse[2:4, 0:AC], coarse[0:2, 0:AC])
    q_out[...] = jnp.where(odd, q[2:4, 0:AC], q[0:2, 0:AC])


def air_body(
    info, u, v, block, pin, out, second, far, k16, sp, nr, fs,
    air_out,
    strips,
):
    odd = info[0] == 1
    right = info[1] == 1
    r = info[2]
    for i, (ref, lo) in enumerate(((sp, 16), (sp, 24), (nr, 48), (nr, 56), (fs, 48))):
        strips[i] = air_strip(ref, right, lo)
    lanes = lanes_inside(right, 1)
    masks, kd = {}, {}
    for row in range(-3, 5):
        place = r * 2 + row
        masks[row] = lanes * jnp.where((place >= 0) & (place < 512), 1.0, 0.0)
        a, b = (2 + row) % 16, row % 16
        kd[row] = jnp.where(odd, k16[a : a + 1, :], k16[b : b + 1, :]) * masks[row]

    def group(half, g):
        at = pl.multiple_of(g * 8, 8)
        own8 = pl.ds(72 + at, 8)
        out8 = pl.ds(24 + at, 8)

        def whole(ref, rows, lane, strip, i):
            side = strips[strip, pl.ds(32 * half + i * FL + at, 8), :]
            return jnp.concatenate([ref[rows, lane * AC : (lane + 1) * AC], side], axis=1)

        x = {i: whole(block, own8, 2 * half + i, 0, i) for i in range(2)}
        p = [whole(pin, own8, 2 * half + i, 1, i) for i in range(2)]
        o = [whole(out, out8, 2 * half + i, 2, i) for i in range(2)]
        o2 = [whole(second, pl.ds(at, 8), 2 * half + i, 3, i) for i in range(2)]
        f = [whole(far, out8, 2 * half + i, 4, i) for i in range(2)]
        for i in range(2):
            x[2 + i] = jnp.where(odd, o[i], p[i])
            x[4 + i] = jnp.where(odd, o2[i], f[i])
            x[-2 + i] = jnp.where(odd, p[i], o[i])
            x[-4 + i] = jnp.where(odd, f[i], o2[i])
        row8 = lax.broadcasted_iota(jnp.int32, (8, AW), 0)
        hu = jnp.zeros((8, AW), F32)
        hv = jnp.zeros((8, AW), F32)
        for i in range(8):
            hu = jnp.where(row8 == i, 0.5 * u[at + i], hu)
            hv = jnp.where(row8 == i, 0.5 * v[at + i], hv)
        for step in range(ASTEPS * COUPLE):
            new = {}
            for row in range(-3 + step, 5 - step):
                c, n, s = x[row], x[row - 1], x[row + 1]
                w = pltpu.roll(c, 1, 1)
                e = pltpu.roll(c, AW - 1, 1)
                new[row] = (
                    masks[row] * (c - hu * (e - w) - hv * (s - n))
                    + kd[row] * (n + s + w + e - 4.0 * c)
                )
            x = new
        for i in range(2):
            air_out[pl.ds(32 * half + at, 8), i, :] = x[i][:, 0:AC]

    for half in range(2):
        lax.fori_loop(0, 4, lambda g, c, half=half: (group(half, g), c)[1], 0)


def route_body(info, own, got, above, flow_out, hot):
    j = info[3]
    target = lax.broadcasted_iota(jnp.int32, (2 * LINKS, LINKS), 0).astype(F32)
    data = [own[...]] + [got[lax.rem(j - k + 16, 16)] for k in range(1, STEPS + 1)]

    def wide(d, i):
        return jnp.concatenate([d[2 * i : 2 * i + 1, :], d[2 * i + 1 : 2 * i + 2, :]], axis=1)

    flow = [wide(own[...], 8), wide(above[...], 0)] + [wide(d, 6) for d in data[2:]]
    for k in range(STEPS + 1):
        hot[k] = jnp.where(target == wide(data[k], 7 if k else 9), 1.0, 0.0).astype(BF16)
    for t in range(STEPS):
        routed = []
        for k in range(STEPS - t + 1):
            f = flow[k]
            f1 = f.astype(BF16)
            rest = f - f1.astype(F32)
            f2 = rest.astype(BF16)
            f3 = (rest - f2.astype(F32)).astype(BF16)
            lhs = jnp.concatenate([f1, f2, f3, jnp.zeros((13, LINKS), BF16)], axis=0)
            first = 0 if k < STEPS - t else LINKS
            last = 2 * LINKS if k > 0 else LINKS
            y = lax.dot_general(
                lhs,
                hot[k, first:last, :],
                (((1,), (1,)), ((), ())),
                preferred_element_type=F32,
            )
            y = y[0:1] + y[1:2] + y[2:3]
            local = None if first else y[:, 0:LINKS]
            down = y[:, LINKS - first :] if last > LINKS else None
            routed.append((local, down))
        new = []
        for k in range(STEPS - t):
            arrived = routed[k][0] + routed[k + 1][1]
            new.append(flow[k] + 0.5 * (arrived - flow[k]) + wide(data[k], t))
        flow = new
    flow_out[...] = flow[0]


def shards(
    air, kdiff, u_wind, v_wind, elev, cond, rain_factor, land_mask, flow_code,
    depth_init, soil_init, link_cell, link_down, link_flow,
):
    gx = lax.axis_index("gx")
    odd = gx % 2
    row = lax.axis_index("grp") * 16 + gx
    info = jnp.stack([odd, lax.axis_index("gy"), row, gx]).astype(jnp.int32)
    pairs = link_cell.reshape(2, 128), link_flow.reshape(2, 128), link_down.reshape(2, 128)

    land_v = pltpu.VMEM((TR, TC), F32)
    code_v = pltpu.VMEM((TR, TC), jnp.int32)
    block, strip = call(
        pack_body,
        [(BLOCK, TC), (24, 128)],
        [info],
        [air.reshape(FL, 2, AC), kdiff, elev, cond, rain_factor, land_mask, flow_code, depth_init, soil_init,
         link_flow.reshape(1, LINKS)],
        [(1, LINKS), (FL, 2, AC), (2, AC), land_v, land_v, land_v, code_v, code_v, land_v, land_v, (BLOCK, TC), (24, 128),
         pltpu.SemaphoreType.DMA((10,)), pltpu.SemaphoreType.DMA((2,))],
        limit=WHOLE,
        far=2,
    )
    pin = pair_swap(block)
    near, near2 = near_swap(strip), second_shift(strip)
    edge, strips, near = call(
        edge_body, [(EDGE, TC), (64, 128), (32, 128)], [info], [block, pin, near, near2]
    )
    out = chip_swap(edge)
    sp = gy_swap(strips)
    (strips,) = call(pick_body, [(64, 128)], [info], [near, sp])
    far_strips = pair_swap(strips)
    ready, _ = lax.optimization_barrier((out, far_strips))
    far = pair_swap(ready)

    wide, chip, flat = (24, TW), (16, TW), (16, AW)
    (coef, rain_w, static_w, land, ring, soil, lat, q, t, k16, edge, above, sp) = call(
        first_body,
        [(5, 24, TW), wide, wide, chip, wide, chip, (8, 128), flat, flat, flat, (8, TW), (2, 128), (32, 128)],
        [info, u_wind, v_wind],
        [pairs[0], block, pin, out, far, strips, far_strips],
        [(144, TW), wide],
    )
    outb = chip_swap(edge)
    (second,) = call(pair_air_body, [(32, TC)], [], [edge, pin])
    second = chip_swap(second)
    farb = pair_swap(outb)
    depth, coarse, qf, own = call(
        second_body,
        [(TR, TC), (2, AC), (2, AC), (24, 128)],
        [info, u_wind, v_wind],
        [*pairs, coef, rain_w, static_w, land, ring, soil, lat, q, t, k16, outb, farb],
        [wide, chip, wide, flat, flat],
    )
    before = grp_shift(own)
    (chunks,) = call(chunks_body, [(16, 16, 128)], [info], [own, before])
    got = lax.all_to_all(chunks, "gx", 0, 0)
    (air_new,) = call(
        air_body,
        [(FL, 2, AC)],
        [info, u_wind, v_wind],
        [block, pin, out, second, far, k16, sp, strips, far_strips],
        [(5, 128, 128)],
    )
    air_new = air_new.at[Q0].set(qf)

    got, air_new = lax.optimization_barrier((got, air_new))
    (flow,) = call(
        route_body,
        [(1, LINKS)],
        [info],
        [own, got, above],
        [pltpu.VMEM((STEPS + 1, 2 * LINKS, LINKS), BF16)],
    )
    return (air_new.reshape(2, 32, 2, AC), depth, coarse, flow.reshape(LINKS))


def solution(mesh):
    placed = (
        P(None, None, ("grp", "gx"), "gy"),
        P(("grp", "gx"), "gy"),
        P(),
        P(),
        P(("grp", "gx"), "gy"),
        P(("grp", "gx"), "gy"),
        P(("grp", "gx"), "gy"),
        P(("grp", "gx"), "gy"),
        P(("grp", "gx"), "gy"),
        P(("grp", "gx"), "gy"),
        P(("grp", "gx"), "gy"),
        P(AXES),
        P(AXES),
        P(AXES),
    )
    return jax.shard_map(
        shards,
        mesh=mesh,
        in_specs=placed,
        out_specs=(
            P(None, None, ("grp", "gx"), "gy"),
            P(("grp", "gx"), "gy"),
            P(("grp", "gx"), "gy"),
            P(AXES),
        ),
        check_vma=False,
    )
```

```python
import jax
import jax.numpy as jnp
from jax import lax
from jax.experimental import pallas as pl
from jax.experimental.pallas import tpu as pltpu
from jax.sharding import PartitionSpec as P

ASTEPS = 2
HSTEPS = 4
COUPLE = 2
STEPS = HSTEPS * COUPLE

F32 = jnp.float32
BF16 = jnp.bfloat16
AXES = ("grp", "gx", "gy")
ROOM = 16 * 1024 * 1024
WHOLE = 60 * 1024 * 1024

LINKS = 256
TR = 8
TC = 3072
TW = TC + 128
AC = 768
AW = AC + 128
FL = 64
Q0 = 32


def exchange(value, partner):
    pairs = []
    for r in range(256):
        for g in range(2):
            t, h = partner(r, g)
            if 0 <= t < 256:
                pairs.append((r * 2 + g, t * 2 + h))
    return lax.ppermute(value, AXES, pairs)


def outer(r):
    return r + 1 if r % 2 else r - 1


def pair_swap(value):
    return exchange(value, lambda r, g: (r ^ 1, g))


def chip_swap(value):
    return exchange(value, lambda r, g: (outer(r), g))


def beside(r, t, g):
    return (t, g if t // 16 == r // 16 else 1 - g)


def near_swap(value):
    return exchange(value, lambda r, g: beside(r, outer(r), g))


def second_shift(value):
    return exchange(value, lambda r, g: beside(r, r - 2 if r % 2 else r + 2, g))


def gy_swap(value):
    return exchange(value, lambda r, g: (r if 0 < r % 16 < 15 else -1, 1 - g))


def grp_shift(value):
    return exchange(value, lambda r, g: (r + 16, g))


def vmem():
    return pl.BlockSpec(memory_space=pltpu.VMEM)


def smem():
    return pl.BlockSpec(memory_space=pltpu.SMEM)


def hbm():
    return pl.BlockSpec(memory_space=pltpu.HBM)


def call(body, outs, scalars, arrays, scratch=(), limit=ROOM, far=0):
    space = hbm() if far else vmem()
    return pl.pallas_call(
        body,
        out_shape=[jax.ShapeDtypeStruct(o, F32) for o in outs],
        in_specs=[smem()] * len(scalars) + [space] * len(arrays),
        out_specs=[hbm() if i < far else vmem() for i in range(len(outs))],
        scratch_shapes=[pltpu.VMEM(x, F32) if isinstance(x, tuple) else x for x in scratch],
        compiler_params=pltpu.CompilerParams(vmem_limit_bytes=limit),
    )(*scalars, *arrays)


BLOCK, EDGE = 104, 56
ELEV, COND, RAIN, MASK, CODE, DEPTH, SOIL = range(7)
EDGES = ((ELEV, 0, 4), (COND, 12, 3), (RAIN, 15, 3), (MASK, 18, 3), (CODE, 4, 4), (DEPTH, 8, 4))


def pack_body(
    info, air, kd, elev, cond, rf, mask, code, depth, soil, links,
    block_h, strip_h,
    links_v, air_v, kd_v, elev_v, cond_v, rf_v, mask_v, code_v, depth_v, soil_v,
    block, strip, sems, sent,
):
    right = info[1] == 1
    near = (kd_v, elev_v, cond_v, rf_v, mask_v, code_v, depth_v, soil_v, air_v, links_v)
    copies = [
        pltpu.make_async_copy(src, dst, sems.at[i])
        for i, (src, dst) in enumerate(
            zip((kd, elev, cond, rf, mask, code, depth, soil, air, links), near)
        )
    ]
    for c in copies:
        c.start()
    block[56:72, :] = jnp.zeros((16, TC), F32)
    parts = ((block.at[0:56], block_h.at[0:56]), (block.at[72:104], block_h.at[72:104]),
             (block.at[56:72], block_h.at[56:72]), (strip, strip_h))
    results = [pltpu.make_async_copy(a, b, sent.at[i]) for i, (a, b) in enumerate(parts)]
    for i, ref in enumerate((elev_v, cond_v, rf_v, mask_v, code_v, depth_v, soil_v)):
        copies[i + 1].wait()
        block[8 * i : 8 * i + 8, :] = ref[...].astype(F32)
    results[0].start()
    for i in (0, 8, 9):
        copies[i].wait()
    block[58:59, 0:LINKS] = links_v[...]
    ends = []
    for r in range(2):
        rows = air_v[:, r, :]
        for h in range(2):
            at = slice((2 * h + r) * AC, (2 * h + r + 1) * AC)
            block[72:104, at] = rows[32 * h : 32 * h + 32, :]
        block[56:57, r * AC : (r + 1) * AC] = rows[Q0 : Q0 + 1, :]
        block[56:57, (2 + r) * AC : (3 + r) * AC] = rows[0:1, :]
        block[57:58, r * AC : (r + 1) * AC] = kd_v[r : r + 1, :]
        ends.append(jnp.where(right, rows[:, 0:128], rows[:, AC - 128 : AC]))
    results[1].start()
    land = jnp.where(right, block[0:56, 0:128], block[0:56, TC - 128 : TC])
    kblock = jnp.where(right, kd_v[:, 0:128], kd_v[:, AC - 128 : AC])
    square = jnp.concatenate([land, kblock, jnp.zeros((70, 128), F32)], axis=0).T
    strip[0:16, :] = jnp.where(right, square[0:16], square[112:128])
    ablock = jnp.concatenate(ends, axis=0).T
    strip[16:24, :] = jnp.where(right, ablock[0:8], ablock[120:128])
    for b in range(3):
        block[64:72, b * 128 : (b + 1) * 128] = strip[8 * b : 8 * b + 8, :]
    results[2].start()
    results[3].start()
    for c in results:
        c.wait()


def edge_body(info, block, pin, near, near2, out, strips, beyond):
    odd = info[0] == 1
    for i, off, n in EDGES:
        top = block[8 * i : 8 * i + n, :]
        low = block[8 * i + 8 - n : 8 * i + 8, :]
        out[off : off + n, :] = jnp.where(odd, low, top)
    out[21:24, :] = block[56:59, :]
    for i in range(2):
        a = pin[56 + i : 57 + i, AC : 2 * AC]
        b = pin[56 + i : 57 + i, 0:AC]
        out[22:23, (2 + i) * AC : (3 + i) * AC] = jnp.where(odd, a, b)
    out[24:56, :] = block[72:104, :]
    lane = lax.broadcasted_iota(jnp.int32, (8, 128), 1)
    for b in range(2):
        at, rows = slice(b * 128, (b + 1) * 128), slice(8 * b, 8 * b + 8)
        pair = pltpu.roll(pin[64:72, at], 64, 1)
        strips[rows, :] = jnp.where(lane < 64, block[64:72, at], pair)
        beyond[rows, :] = jnp.where(lane < 64, near[rows, :], pltpu.roll(near2[rows, :], 64, 1))
    strips[16:24, :] = block[64:72, 256:384]
    strips[24:32, :] = pin[64:72, 256:384]
    beyond[16:24, :] = near[16:24, :]
    beyond[24:32, :] = near2[16:24, :]
    strips[32:64, :] = beyond[...]


def pair_air_body(edge, pin, out):
    out[...] = pin[72:104, :]


def pick_body(info, near, across, out):
    end = (info[3] == 0) | (info[3] == 15)
    out[0:32, :] = across[0:32, :]
    out[32:64, :] = jnp.where(end, near[...], across[32:64, :])


def chunks_body(info, own, before, out):
    for i in range(16):
        src = jnp.where(info[3] < i, own[...], before[...])
        out[i, 0:12, :] = src[0:12]
        out[i, 12:14, :] = jnp.where(info[3] == (i + 15) % 16, src[12:14], src[16:18])
        out[i, 14:16, :] = src[18:20]


def land_strip(strip, right):
    zero = jnp.zeros((112, 128), F32)
    s = strip[0:16, :]
    return jnp.where(
        right, jnp.concatenate([zero, s], axis=0), jnp.concatenate([s, zero], axis=0)
    ).T


def air_strip(strip, right, lo):
    zero = jnp.zeros((120, 128), F32)
    s = strip[lo : lo + 8, :]
    return jnp.where(
        right, jnp.concatenate([zero, s], axis=0), jnp.concatenate([s, zero], axis=0)
    ).T


def lanes_inside(right, rows):
    lane = lax.broadcasted_iota(jnp.int32, (rows, AW), 1)
    edge = jnp.where(right, AW - 8, AC)
    halo = (lane >= edge) & (lane < edge + 8)
    return jnp.where((lane < AC) | halo, 1.0, 0.0).astype(F32)


def ring_mask(info, right):
    row = lax.broadcasted_iota(jnp.int32, (16, AW), 0)
    place = (info[2] - info[0]) * 2 + jnp.where(row < 8, row, row - 16)
    return jnp.where((place >= 0) & (place < 512), lanes_inside(right, 16), 0.0)


def ring_step(x, k, m, hu, hv):
    n = pltpu.roll(x, 1, 0)
    s = pltpu.roll(x, 15, 0)
    w = pltpu.roll(x, 1, 1)
    e = pltpu.roll(x, AW - 1, 1)
    return m * (x + k * (n + s + w + e - 4.0 * x) - hu * (e - w) - hv * (s - n))


def spread_matrix():
    i = lax.broadcasted_iota(jnp.int32, (128, 512), 0)
    j = lax.broadcasted_iota(jnp.int32, (128, 512), 1)
    return jnp.where(j // 4 == i, 1.0, 0.0).astype(BF16)


def two_parts(x):
    high = x.astype(BF16)
    low = (x - high.astype(F32)).astype(BF16)
    return jnp.concatenate([high, low], axis=0)


def spread_columns(rain, right):
    blocks = jnp.concatenate([rain[:, 128 * b : 128 * b + 128] for b in range(7)], axis=0)
    wide = jnp.dot(two_parts(blocks), spread_matrix(), preferred_element_type=F32)
    wide = wide[0:112] + wide[112:224]
    parts = [wide[16 * b : 16 * b + 16] for b in range(6)]
    last = wide[96:112]
    parts.append(jnp.where(right, last[:, 384:512], last[:, 0:128]))
    return jnp.concatenate(parts, axis=1)


def spread_rows(wide):
    row = lax.broadcasted_iota(jnp.int32, (8, TW), 0)
    return jnp.concatenate(
        [
            jnp.where(row < 4, wide[a : a + 1, :], wide[b : b + 1, :])
            for a, b in ((0, 1), (2, 3), (4, 15))
        ],
        axis=0,
    )


def soil_mean(soil, right):
    zero = jnp.zeros((16, 384), F32)
    last = soil[:, TC:TW]
    last = jnp.where(
        right,
        jnp.concatenate([zero, last], axis=1),
        jnp.concatenate([last, zero], axis=1),
    )
    blocks = jnp.concatenate([soil[:, 512 * b : 512 * b + 512] for b in range(6)] + [last], axis=0)
    sums = lax.dot_general(
        two_parts(blocks),
        spread_matrix(),
        (((1,), (1,)), ((), ())),
        preferred_element_type=F32,
    )
    sums = sums[0:112] + sums[112:224]
    wide = jnp.concatenate([sums[16 * b : 16 * b + 16] for b in range(7)], axis=1)
    wide = wide + pltpu.roll(wide, 15, 0)
    wide = wide + pltpu.roll(wide, 14, 0)
    row = lax.broadcasted_iota(jnp.int32, (16, AW), 0)
    mean = jnp.zeros((16, AW), F32)
    for i in range(4):
        mean = jnp.where(row == i, wide[4 * i : 4 * i + 1, :], mean)
    return mean * 0.0625


def lateral_of(depth, cells):
    row = lax.broadcasted_iota(jnp.int32, (8, 128), 0) * (TC // 128)
    out = []
    for h in range(2):
        cell = cells[h : h + 1, :]
        lane = jnp.broadcast_to(cell % 128, (8, 128))
        block = jnp.broadcast_to(cell // 128, (8, 128)) - row
        total = jnp.zeros((8, 128), F32)
        for b in range(TC // 128):
            got = jnp.take_along_axis(depth[:, 128 * b : 128 * b + 128], lane, axis=1)
            total = jnp.where(block == b, got, total)
        out.append(0.1 * jnp.sum(total, axis=0, keepdims=True))
    return out


def hydro(odd, coef, rq, ring, land, soil, cells, lat, base):
    for t in range(HSTEPS):
        d = ring[...]
        halves = lateral_of(jnp.where(odd, ring[8:16, 0:TC], ring[0:8, 0:TC]), cells)
        for h in range(2):
            lat[base + 2 * t + h : base + 2 * t + h + 1, :] = halves[h]
        soil[...] = soil[...] + 0.05 * land[...] * d[0:16] - 0.02 * soil[...]
        new = rq[...] + coef[0] * d
        new = new + coef[1] * pltpu.roll(d, 1, 1)
        new = new + coef[2] * pltpu.roll(d, TW - 1, 1)
        new = new + coef[3] * pltpu.roll(d, 1, 0)
        new = new + coef[4] * pltpu.roll(d, 23, 0)
        ring[...] = new


def rain_of(q):
    rain = 0.05 * q * q
    return rain, q - rain


def first_body(
    info, u, v, cells, block, pin, out, far, strips, far_strips,
    coef, rain_w, static_w, land, ring, soil, lat, q_out, t_out, k_out, edge, above, sp,
    grid, rq,
):
    odd = info[0] == 1
    right = info[1] == 1
    hu_t, hv_t = 0.5 * u[0], 0.5 * v[0]
    end = (info[3] == 0) | (info[3] == 15)
    sp[0:16, :] = jnp.where(end, pltpu.roll(far_strips[0:16, :], 64, 1), strips[0:16, :])
    sp[16:24, :] = jnp.where(end, far_strips[24:32, :], strips[16:24, :])
    sp[24:32, :] = jnp.where(end, far_strips[16:24, :], strips[24:32, :])
    nr, fs = strips.at[32:64, :], far_strips.at[32:64, :]
    square = land_strip(sp, right)
    mine, pair = square[0:64], square[64:128]
    cols = (jnp.where(odd, pair, mine), jnp.where(odd, mine, pair))
    square = land_strip(nr, right)
    beyond, out2 = square[0:64], square[64:128]
    square = land_strip(fs, right)
    other, far2 = square[0:64], square[64:128]
    cols_s, cols_n = jnp.where(odd, beyond, other), jnp.where(odd, other, beyond)
    grid[...] = jnp.zeros_like(grid)

    def chip_rows(ref, i, lo):
        at = slice(8 * i, 8 * i + 8)
        ref[lo : lo + 8, 0:TC] = jnp.where(odd, pin[at, :], block[at, :])
        ref[lo + 8 : lo + 16, 0:TC] = jnp.where(odd, block[at, :], pin[at, :])
        ref[lo : lo + 8, TC:TW] = cols[0][at]
        ref[lo + 8 : lo + 16, TC:TW] = cols[1][at]

    for i, off, n in EDGES:
        chip_rows(grid, i, 24 * i)
        e_out = out[off : off + n, :]
        e_far = far[off : off + n, :]
        lo = 24 * i
        grid[lo + 16 : lo + 16 + n, 0:TC] = jnp.where(odd, e_out, e_far)
        grid[lo + 24 - n : lo + 24, 0:TC] = jnp.where(odd, e_far, e_out)
        grid[lo + 16 : lo + 16 + n, TC:TW] = cols_s[8 * i : 8 * i + n]
        grid[lo + 24 - n : lo + 24, TC:TW] = cols_n[8 * i + 8 - n : 8 * i + 8]
    chip_rows(soil, SOIL, 0)

    def field(i):
        return grid[24 * i : 24 * i + 24, :]

    m = field(MASK)
    land[...] = m[0:16]
    eta = field(ELEV)
    lap = (
        pltpu.roll(eta, 1, 1)
        + pltpu.roll(eta, TW - 1, 1)
        + pltpu.roll(eta, 1, 0)
        + pltpu.roll(eta, 23, 0)
        - 4.0 * eta
    )
    mc = m * field(COND)
    codes = field(CODE)
    share = 0.2 * m
    coef[0] = 0.75 * m - 4.0 * mc
    coef[1] = mc + jnp.where(pltpu.roll(codes, 1, 1) == 0.0, share, 0.0)
    coef[2] = mc + jnp.where(pltpu.roll(codes, TW - 1, 1) == 2.0, share, 0.0)
    coef[3] = mc + jnp.where(pltpu.roll(codes, 1, 0) == 3.0, share, 0.0)
    coef[4] = mc + jnp.where(pltpu.roll(codes, 23, 0) == 1.0, share, 0.0)
    rain_w[...] = m * field(RAIN)
    static_w[...] = mc * lap
    ring[...] = field(DEPTH)
    mine_a, pair_a = air_strip(sp, right, 16), air_strip(sp, right, 24)
    out_a, out2_a = air_strip(nr, right, 16), air_strip(nr, right, 24)
    far_a, far2_a = air_strip(fs, right, 16), air_strip(fs, right, 24)
    own_r, pair_r = block[56:64, :], pin[56:64, :]
    out_r, far_r = out[16:24, :], far[16:24, :]
    for ref in (q_out, t_out, k_out):
        ref[...] = jnp.zeros_like(ref)
    for odd_side, msg, first, air_s, col_s in (
        (None, jnp.where(odd, pair_r, own_r), 0, jnp.where(odd, pair_a, mine_a), cols[0]),
        (None, jnp.where(odd, own_r, pair_r), 2, jnp.where(odd, mine_a, pair_a), cols[1]),
        (False, jnp.where(odd, out_r, far_r), 4, jnp.where(odd, out_a, far_a), cols_s),
        (True, jnp.where(odd, far_r, out_r), 14, jnp.where(odd, far_a, out_a), cols_n),
    ):
        top = 0 if odd_side is None else 5
        for i in range(2):
            at = slice(first + i, first + i + 1)
            q_out[at, 0:AC] = msg[top : top + 1, i * AC : (i + 1) * AC]
            t_out[at, 0:AC] = msg[top : top + 1, (2 + i) * AC : (3 + i) * AC]
            k_out[at, 0:AC] = msg[top + 1 : top + 2, i * AC : (i + 1) * AC]
            q_out[at, AC:AW] = air_s[i * FL + Q0 : i * FL + Q0 + 1]
            t_out[at, AC:AW] = air_s[i * FL : i * FL + 1]
            k_out[at, AC:AW] = col_s[56 + i : 57 + i]
        if odd_side is not None:
            place = 13 if odd_side else 6
            i = 1 if odd_side else 0
            at = slice(place, place + 1)
            third_a = jnp.where(odd, far2_a, out2_a) if odd_side else jnp.where(odd, out2_a, far2_a)
            third = jnp.where(odd, far2, out2) if odd_side else jnp.where(odd, out2, far2)
            q_out[at, 0:AC] = msg[6:7, 2 * AC : 3 * AC]
            k_out[at, 0:AC] = msg[6:7, 3 * AC : 4 * AC]
            q_out[at, AC:AW] = third_a[i * FL + Q0 : i * FL + Q0 + 1]
            k_out[at, AC:AW] = third[56 + i : 57 + i]
    m8 = ring_mask(info, right)
    k = k_out[...]
    q, t = q_out[...], t_out[...]
    for _ in range(ASTEPS):
        q = ring_step(q, k, m8, hu_t, hv_t)
        t = ring_step(t, k, m8, hu_t, hv_t)
    for h in range(2):
        at = slice(128 * h, 128 * h + 128)
        above[h : h + 1, :] = jnp.where(odd, pin[58:59, at], out[23:24, at])
    rain, q = rain_of(q)
    rq[...] = static_w[...] + rain_w[...] * spread_rows(spread_columns(rain, right))
    lat[...] = jnp.zeros_like(lat)
    hydro(odd, coef, rq, ring, land, soil, cells[...], lat, 0)
    q = q + 0.1 * soil_mean(soil[...], right) * jax.nn.sigmoid(t)
    q_out[...] = q
    t_out[...] = t
    edge[0:4, :] = jnp.where(odd, ring[12:16, :], ring[0:4, :])
    edge[4:8, :] = jnp.zeros((4, TW), F32)
    for lane, a, b in ((0, 2, 0), (1, 3, 1), (2, 1, 2)):
        at = slice(lane * AW, (lane + 1) * AW)
        edge[4:5, at] = jnp.where(odd, q[a : a + 1], q[b : b + 1])
        if lane < 2:
            edge[5:6, at] = jnp.where(odd, t[a : a + 1], t[b : b + 1])


def second_body(
    info, u, v, cells, link_flow, link_down, coef, rain_w, static_w, land, ring0, soil0, lat0,
    q0, t0, k0, out, far,
    depth_out, coarse_out, q_out, lat,
    ring, soil, rq, q8, t8,
):
    odd = info[0] == 1
    right = info[1] == 1
    hu_t, hv_t = 0.5 * u[0], 0.5 * v[0]
    ring[0:16, :] = ring0[0:16, :]
    south = jnp.where(odd, out[...], far[...])
    north = jnp.where(odd, far[...], out[...])
    ring[16:20, :] = south[0:4]
    ring[20:24, :] = north[0:4]
    soil[...] = soil0[...]
    q8[...] = jnp.zeros_like(q8)
    t8[...] = jnp.zeros_like(t8)
    q8[0:4, :] = q0[0:4, :]
    t8[0:4, :] = t0[0:4, :]
    for places, msg in (((4, 5, 6), south), ((14, 15, 13), north)):
        for i, place in enumerate(places):
            q8[place : place + 1, :] = msg[4:5, i * AW : (i + 1) * AW]
            if i < 2:
                t8[place : place + 1, :] = msg[5:6, i * AW : (i + 1) * AW]
    m8 = ring_mask(info, right)
    k = k0[...]
    q, t = q8[...], t8[...]
    for _ in range(ASTEPS):
        q = ring_step(q, k, m8, hu_t, hv_t)
        t = ring_step(t, k, m8, hu_t, hv_t)
    rain, q = rain_of(q)
    rq[...] = static_w[...] + rain_w[...] * spread_rows(spread_columns(rain, right))
    lat[0:8, :] = lat0[...]
    lat[16:24, :] = jnp.zeros((8, 128), F32)
    lat[16:18, :] = link_flow[...]
    lat[18:20, :] = link_down[...].astype(F32)
    hydro(odd, coef, rq, ring, land, soil, cells[...], lat, 8)
    coarse = soil_mean(soil[...], right)
    q = q + 0.1 * coarse * jax.nn.sigmoid(t)
    depth_out[...] = jnp.where(odd, ring[8:16, 0:TC], ring[0:8, 0:TC])
    coarse_out[...] = jnp.where(odd, coarse[2:4, 0:AC], coarse[0:2, 0:AC])
    q_out[...] = jnp.where(odd, q[2:4, 0:AC], q[0:2, 0:AC])


def air_body(
    info, u, v, block, pin, out, second, far, k16, sp, nr, fs,
    air_out,
    strips,
):
    odd = info[0] == 1
    right = info[1] == 1
    r = info[2]
    for i, (ref, lo) in enumerate(((sp, 16), (sp, 24), (nr, 48), (nr, 56), (fs, 48))):
        strips[i] = air_strip(ref, right, lo)
    lanes = lanes_inside(right, 1)
    masks, kd = {}, {}
    for row in range(-3, 5):
        place = r * 2 + row
        masks[row] = lanes * jnp.where((place >= 0) & (place < 512), 1.0, 0.0)
        a, b = (2 + row) % 16, row % 16
        kd[row] = jnp.where(odd, k16[a : a + 1, :], k16[b : b + 1, :]) * masks[row]

    def group(half, g):
        at = pl.multiple_of(g * 8, 8)
        own8 = pl.ds(72 + at, 8)
        out8 = pl.ds(24 + at, 8)

        def whole(ref, rows, lane, strip, i):
            side = strips[strip, pl.ds(32 * half + i * FL + at, 8), :]
            return jnp.concatenate([ref[rows, lane * AC : (lane + 1) * AC], side], axis=1)

        x = {i: whole(block, own8, 2 * half + i, 0, i) for i in range(2)}
        p = [whole(pin, own8, 2 * half + i, 1, i) for i in range(2)]
        o = [whole(out, out8, 2 * half + i, 2, i) for i in range(2)]
        o2 = [whole(second, pl.ds(at, 8), 2 * half + i, 3, i) for i in range(2)]
        f = [whole(far, out8, 2 * half + i, 4, i) for i in range(2)]
        for i in range(2):
            x[2 + i] = jnp.where(odd, o[i], p[i])
            x[4 + i] = jnp.where(odd, o2[i], f[i])
            x[-2 + i] = jnp.where(odd, p[i], o[i])
            x[-4 + i] = jnp.where(odd, f[i], o2[i])
        row8 = lax.broadcasted_iota(jnp.int32, (8, AW), 0)
        hu = jnp.zeros((8, AW), F32)
        hv = jnp.zeros((8, AW), F32)
        for i in range(8):
            hu = jnp.where(row8 == i, 0.5 * u[at + i], hu)
            hv = jnp.where(row8 == i, 0.5 * v[at + i], hv)
        for step in range(ASTEPS * COUPLE):
            new = {}
            for row in range(-3 + step, 5 - step):
                c, n, s = x[row], x[row - 1], x[row + 1]
                w = pltpu.roll(c, 1, 1)
                e = pltpu.roll(c, AW - 1, 1)
                new[row] = (
                    masks[row] * (c - hu * (e - w) - hv * (s - n))
                    + kd[row] * (n + s + w + e - 4.0 * c)
                )
            x = new
        for i in range(2):
            air_out[pl.ds(32 * half + at, 8), i, :] = x[i][:, 0:AC]

    for half in range(2):
        lax.fori_loop(0, 4, lambda g, c, half=half: (group(half, g), c)[1], 0)


def route_body(info, own, got, above, flow_out, hot):
    j = info[3]
    target = lax.broadcasted_iota(jnp.int32, (2 * LINKS, LINKS), 0).astype(F32)
    data = [own[...]] + [got[lax.rem(j - k + 16, 16)] for k in range(1, STEPS + 1)]

    def wide(d, i):
        return jnp.concatenate([d[2 * i : 2 * i + 1, :], d[2 * i + 1 : 2 * i + 2, :]], axis=1)

    flow = [wide(own[...], 8), wide(above[...], 0)] + [wide(d, 6) for d in data[2:]]
    for k in range(STEPS + 1):
        hot[k] = jnp.where(target == wide(data[k], 7 if k else 9), 1.0, 0.0).astype(BF16)
    for t in range(STEPS):
        routed = []
        for k in range(STEPS - t + 1):
            f = flow[k]
            f1 = f.astype(BF16)
            rest = f - f1.astype(F32)
            f2 = rest.astype(BF16)
            f3 = (rest - f2.astype(F32)).astype(BF16)
            lhs = jnp.concatenate([f1, f2, f3, jnp.zeros((13, LINKS), BF16)], axis=0)
            first = 0 if k < STEPS - t else LINKS
            last = 2 * LINKS if k > 0 else LINKS
            y = lax.dot_general(
                lhs,
                hot[k, first:last, :],
                (((1,), (1,)), ((), ())),
                preferred_element_type=F32,
            )
            y = y[0:1] + y[1:2] + y[2:3]
            local = None if first else y[:, 0:LINKS]
            down = y[:, LINKS - first :] if last > LINKS else None
            routed.append((local, down))
        new = []
        for k in range(STEPS - t):
            arrived = routed[k][0] + routed[k + 1][1]
            new.append(flow[k] + 0.5 * (arrived - flow[k]) + wide(data[k], t))
        flow = new
    flow_out[...] = flow[0]


def shards(
    air, kdiff, u_wind, v_wind, elev, cond, rain_factor, land_mask, flow_code,
    depth_init, soil_init, link_cell, link_down, link_flow,
):
    gx = lax.axis_index("gx")
    odd = gx % 2
    row = lax.axis_index("grp") * 16 + gx
    info = jnp.stack([odd, lax.axis_index("gy"), row, gx]).astype(jnp.int32)
    pairs = link_cell.reshape(2, 128), link_flow.reshape(2, 128), link_down.reshape(2, 128)

    land_v = pltpu.VMEM((TR, TC), F32)
    code_v = pltpu.VMEM((TR, TC), jnp.int32)
    block, strip = call(
        pack_body,
        [(BLOCK, TC), (24, 128)],
        [info],
        [air.reshape(FL, 2, AC), kdiff, elev, cond, rain_factor, land_mask, flow_code, depth_init, soil_init,
         link_flow.reshape(1, LINKS)],
        [(1, LINKS), (FL, 2, AC), (2, AC), land_v, land_v, land_v, code_v, code_v, land_v, land_v, (BLOCK, TC), (24, 128),
         pltpu.SemaphoreType.DMA((10,)), pltpu.SemaphoreType.DMA((4,))],
        limit=WHOLE,
        far=2,
    )
    pin = pair_swap(block)
    near, near2 = near_swap(strip), second_shift(strip)
    edge, strips, near = call(
        edge_body, [(EDGE, TC), (64, 128), (32, 128)], [info], [block, pin, near, near2]
    )
    out = chip_swap(edge)
    sp = gy_swap(strips)
    (strips,) = call(pick_body, [(64, 128)], [info], [near, sp])
    far_strips = pair_swap(strips)
    ready, _ = lax.optimization_barrier((out, far_strips))
    far = pair_swap(ready)

    wide, chip, flat = (24, TW), (16, TW), (16, AW)
    (coef, rain_w, static_w, land, ring, soil, lat, q, t, k16, edge, above, sp) = call(
        first_body,
        [(5, 24, TW), wide, wide, chip, wide, chip, (8, 128), flat, flat, flat, (8, TW), (2, 128), (32, 128)],
        [info, u_wind, v_wind],
        [pairs[0], block, pin, out, far, strips, far_strips],
        [(144, TW), wide],
    )
    outb = chip_swap(edge)
    (second,) = call(pair_air_body, [(32, TC)], [], [edge, pin])
    second = chip_swap(second)
    farb = pair_swap(outb)
    depth, coarse, qf, own = call(
        second_body,
        [(TR, TC), (2, AC), (2, AC), (24, 128)],
        [info, u_wind, v_wind],
        [*pairs, coef, rain_w, static_w, land, ring, soil, lat, q, t, k16, outb, farb],
        [wide, chip, wide, flat, flat],
    )
    before = grp_shift(own)
    (chunks,) = call(chunks_body, [(16, 16, 128)], [info], [own, before])
    got = lax.all_to_all(chunks, "gx", 0, 0)
    (air_new,) = call(
        air_body,
        [(FL, 2, AC)],
        [info, u_wind, v_wind],
        [block, pin, out, second, far, k16, sp, strips, far_strips],
        [(5, 128, 128)],
    )
    air_new = air_new.at[Q0].set(qf)

    got, air_new = lax.optimization_barrier((got, air_new))
    (flow,) = call(
        route_body,
        [(1, LINKS)],
        [info],
        [own, got, above],
        [pltpu.VMEM((STEPS + 1, 2 * LINKS, LINKS), BF16)],
    )
    return (air_new.reshape(2, 32, 2, AC), depth, coarse, flow.reshape(LINKS))


def solution(mesh):
    placed = (
        P(None, None, ("grp", "gx"), "gy"),
        P(("grp", "gx"), "gy"),
        P(),
        P(),
        P(("grp", "gx"), "gy"),
        P(("grp", "gx"), "gy"),
        P(("grp", "gx"), "gy"),
        P(("grp", "gx"), "gy"),
        P(("grp", "gx"), "gy"),
        P(("grp", "gx"), "gy"),
        P(("grp", "gx"), "gy"),
        P(AXES),
        P(AXES),
        P(AXES),
    )
    return jax.shard_map(
        shards,
        mesh=mesh,
        in_specs=placed,
        out_specs=(
            P(None, None, ("grp", "gx"), "gy"),
            P(("grp", "gx"), "gy"),
            P(("grp", "gx"), "gy"),
            P(AXES),
        ),
        check_vma=False,
    )
```
